32 devices in a mesh: row: 4 (over y, core), col: 8 (over z, x).
Axes of the slice: x: 2, y: 2, z: 4, core: 2. Of those that a mesh axis runs over, the one named last changes fastest.
Arguments:
- tangent: bfloat16 [4, 8, 64, 4096], P('row', 'col')
- block_row: int32 [4, 8, 64], P('row', 'col'), may hold values from 0 to 15
- block_col: int32 [4, 8, 64], P('row', 'col'), may hold values from 0 to 7
- tile_count: int32 [4, 8], P('row', 'col'), may hold values from 1 to 64, 320 in all within a row
- old_basis: bfloat16 [64, 3072], P(('row', 'col'))
- old_id: int32 [64], P(('row', 'col')), may hold values from 0 to 63, as said below
- residual: float32 [4096], P(('row', 'col'))
Outputs:
- recycled_c: bfloat16 [64, 3072], P(('row', 'col'))
- recycled_u: bfloat16 [64, 3072], P(('row', 'col'))
- coefficients: float32 [48], replicated
The draws below stay inside these ranges and needn't reach their ends.
Inputs may be any that keep to these rules, and one draw needn't show every extreme that they name: old_id is a permutation of the block rows. Write slot s = (16 * r + 2 * c + i) with 0 <= c < 8 and 0 <= i < 2, and p = i // 2. Its new block row is 16 * r + 2 * ((c + p + 1) mod (8)) + 2 * p + e, with e 0 or 1, the two slots of a pair taking different e. In each row of tile_count the largest count is exactly 64.
All inputs are finite; a program needn't handle non-finite values. No bound on the sum of `tile_count` on one device may be relied on, other than what follows from the above.
Results may differ from the reference program's by a relative error of at most 0.0012.
Values may be sent and summed in bfloat16 or wider, within the bound.
A program may use at most 64 MiB of HBM per device.

```python
import math
import jax
import jax.numpy as jnp
import numpy as np
from jax import lax

BLK = 64
K = 48
RB_DEV = 2
NNZ = 64
NB = 64
TR = 16
TC = 8
N_ROW = 4
N_COL = 8


def draw_tangent(key, part):
    row_groups = NB // TR
    col_groups = TR // RB_DEV
    shape = (row_groups, col_groups, NNZ, BLK, BLK)
    noise = jax.random.normal(jax.random.fold_in(key, 13), shape, jnp.float32)
    row_scale = jnp.exp(jax.random.uniform(jax.random.fold_in(key, 14), (row_groups, 1, 1, BLK, 1), jnp.float32, 0.0, math.log(10.0)))
    rising = jnp.exp(math.log(3.0) * jnp.arange(row_groups, dtype=jnp.float32) / max(row_groups - 1, 1))
    rising = rising.reshape(row_groups, 1, 1, 1, 1)
    per_row = NNZ / TR
    fan_scale = 1.0 / math.sqrt(16.0 * per_row * BLK * col_groups)
    values = noise * row_scale * rising * fan_scale
    return values.reshape(row_groups, col_groups, NNZ, BLK * BLK).astype(jnp.bfloat16)


def draw_old_basis(key, part):
    shape = (NB, BLK, K)
    col_scale = jnp.exp(jax.random.uniform(jax.random.fold_in(key, 21), (1, 1, K), jnp.float32, 0.0, math.log(10.0)))
    noise = jax.random.normal(jax.random.fold_in(key, 24), shape, jnp.float32)
    return (noise * col_scale).reshape(NB, BLK * K).astype(jnp.bfloat16)


def draw_old_id(key, part):
    row_groups = NB // TR
    col_groups = TR // RB_DEV
    pairs = RB_DEV // 2
    flips = jax.random.randint(jax.random.fold_in(key, 32), (row_groups, col_groups, pairs, 1), 0, 2)
    halves = jnp.arange(2, dtype=jnp.int32).reshape(1, 1, 1, 2)
    pair_ids = jnp.arange(pairs, dtype=jnp.int32).reshape(1, 1, pairs, 1)
    col_ids = jnp.arange(col_groups, dtype=jnp.int32).reshape(1, col_groups, 1, 1)
    dest_col = (col_ids + pair_ids + 1) % col_groups
    new_slot = 2 * pair_ids + (halves + flips) % 2
    group_ids = jnp.arange(row_groups, dtype=jnp.int32).reshape(row_groups, 1, 1, 1)
    ids = (group_ids * col_groups + dest_col) * RB_DEV + new_slot
    return ids.reshape(NB).astype(jnp.int32)


def draw_residual(key, part):
    total = NB * BLK
    position = jnp.arange(total, dtype=jnp.float32) / total
    rising = jnp.exp(math.log(3.0) * position)
    block_scale = jnp.exp(jax.random.uniform(jax.random.fold_in(key, 41), (NB, 1), jnp.float32, 0.0, math.log(10.0)))
    block_scale = jnp.broadcast_to(block_scale, (NB, BLK)).reshape(total)
    noise = jax.random.normal(jax.random.fold_in(key, 43), (total,), jnp.float32)
    return noise * rising * block_scale


def set_ends(array, own_key, least, high):
    longest = array.shape.index(max(array.shape))
    spots = []
    for shift in (0, 1):
        where = [jax.random.randint(jax.random.fold_in(own_key, axis), (), 0, length) for axis, length in enumerate(array.shape)]
        where[longest] = (where[longest] + shift) % array.shape[longest]
        spots.append(tuple(where))
    return array.at[spots[0]].set(least).at[spots[1]].set(high)


def profile(amount, total, reach, slope):
    portions = [(1 << 20) // math.isqrt(standing ** slope) + 1 for standing in range(2, amount + 1)]
    spare, given = total - reach - (amount - 1), [1] * (amount - 1)
    while spare > 0:
        candidates = [i for i in range(amount - 1) if given[i] < reach]
        pool, remaining = sum([portions[i] for i in candidates]), spare
        for i in candidates:
            more = min(reach - given[i], max(1, remaining * portions[i] // pool), spare)
            given[i] = given[i] + more
            spare = spare - more
    return np.array([reach] + given)


def ragged(own_key, number_of, total, limit, slope):
    if number_of == 2:
        one = jax.random.randint(own_key, (), max(1, total - limit), min(limit, total - 1) + 1)
        return jnp.stack([one, total - one])
    tallies = jnp.asarray(profile(number_of, total, limit, slope), jnp.int32)
    pairs = (number_of - 1) // 2
    source_of, receiver = tallies[1:1 + 2 * pairs:2], tallies[2:2 + 2 * pairs:2]
    room = jnp.minimum(source_of - 1, limit - receiver)
    shifted = jax.random.randint(jax.random.fold_in(own_key, 1), (pairs,), 0, 1 << 20) % (room + 1)
    tallies = tallies.at[1:1 + 2 * pairs:2].set(source_of - shifted).at[2:2 + 2 * pairs:2].set(receiver + shifted)
    return tallies[jax.random.permutation(jax.random.fold_in(own_key, 2), number_of)]


def setup_inputs(seed: int = 0) -> dict:
    splits = jax.random.split(jax.random.key(seed), 8)
    return {
        "tangent": draw_tangent(jax.random.fold_in(splits[7], 71), 0),
        "block_row": set_ends(jax.random.randint(splits[1], (N_ROW, N_COL, NNZ), 0, TR), jax.random.fold_in(splits[1], 1), 0, TR - 1).astype(jnp.int32),
        "block_col": set_ends(jax.random.randint(splits[2], (N_ROW, N_COL, NNZ), 0, TC), jax.random.fold_in(splits[2], 1), 0, TC - 1).astype(jnp.int32),
        "tile_count": jax.vmap(lambda own: ragged(own, N_COL, NNZ * 5 * N_COL // 8, NNZ, 2))(jax.random.split(splits[3], N_ROW)).reshape((N_ROW, N_COL)).astype(jnp.int32),
        "old_basis": draw_old_basis(jax.random.fold_in(splits[7], 71), 0),
        "old_id": draw_old_id(jax.random.fold_in(splits[7], 71), 0),
        "residual": draw_residual(jax.random.fold_in(splits[7], 71), 0),
    }


def reference(tangent, block_row, block_col, tile_count, old_basis, old_id, residual):
    highest = lax.Precision.HIGHEST
    basis = jnp.zeros_like(old_basis).at[old_id].set(old_basis)
    stacked = basis.reshape(NB, BLK, K)
    tiles = N_ROW * N_COL
    tile_ids = jnp.arange(tiles, dtype=jnp.int32)
    row_ids = tile_ids // N_COL
    col_ids = tile_ids % N_COL
    values = tangent.reshape(tiles, NNZ, BLK, BLK)
    rows_all = block_row.reshape(tiles, NNZ)
    cols_all = block_col.reshape(tiles, NNZ)
    counts = tile_count.reshape(tiles)

    def tile_step(carry, items):
        block_vals, local_rows, local_cols, live_count, row_idx, col_idx = items
        glob_rows = row_idx * TR + local_rows
        glob_cols = (local_cols // RB_DEV * N_COL + col_idx) * RB_DEV + local_cols % RB_DEV
        picked = stacked[glob_cols].astype(jnp.float32)
        prods = jnp.einsum('gij,gjk->gik', block_vals.astype(jnp.float32), picked, precision=highest)
        alive = jnp.arange(NNZ, dtype=jnp.int32) < live_count
        prods = jnp.where(alive[:, None, None], prods, jnp.float32(0.0))
        return (carry.at[glob_rows].add(prods), None)
    product, _ = lax.scan(tile_step, jnp.zeros((NB, BLK, K), jnp.float32), (values, rows_all, cols_all, counts, row_ids, col_ids))
    total_rows = NB * BLK
    flat_c = product.reshape(total_rows, K)
    gram = jnp.dot(flat_c.T, flat_c, precision=highest) / jnp.float32(total_rows)
    lower = jnp.linalg.cholesky(gram)
    ortho_t = jax.scipy.linalg.solve_triangular(lower, flat_c.T, lower=True)
    basis_t = jax.scipy.linalg.solve_triangular(lower, basis.astype(jnp.float32).reshape(total_rows, K).T, lower=True)
    coefficients = jnp.dot(ortho_t, residual, precision=highest) / jnp.float32(math.sqrt(total_rows))
    recycled_c = ortho_t.T.reshape(NB, BLK * K).astype(jnp.bfloat16)
    recycled_u = basis_t.T.reshape(NB, BLK * K).astype(jnp.bfloat16)
    return (recycled_c, recycled_u, coefficients)
```

```python
import functools
import math

import jax
import jax.numpy as jnp
from jax import lax
from jax.experimental import pallas as pl
from jax.experimental.pallas import tpu as pltpu
from jax.sharding import PartitionSpec as P

BLK = 64
K = 48
OCT = BLK // 8
WIDE = 8 * K
SIDE = 64
MESH = pl.DeviceIdType.MESH
F32 = jnp.float32
BF16 = jnp.bfloat16


def iota(shape, dim):
    return lax.broadcasted_iota(jnp.int32, shape, dim)


def over_k(index, most):
    whole = jnp.zeros_like(index)
    for step in range(1, most):
        whole += (index >= K * step).astype(jnp.int32)
    return whole


def pieces(x):
    hi = x.astype(BF16)
    rest = x - hi.astype(F32)
    mid = rest.astype(BF16)
    lo = (rest - mid.astype(F32)).astype(BF16)
    return hi, mid, lo


def kernel(n_row, n_col, tile_rows, tile_cols, tan_hbm, rows_ref, cols_ref, count_ref, basis_ref, id_ref, res_ref,
           c_ref, u_ref, coef_ref,
           tan, xs, xr, w, a, ps, pr, ga, gb,
           tan_sem, bs_send, bs_recv, p_send, p_recv, ga_send, ga_recv, gb_send, gb_recv):
    r = lax.axis_index("row")
    c = lax.axis_index("col")
    nxt = lax.rem(c + 1, n_col)
    prv = lax.rem(c + n_col - 1, n_col)
    small = tile_cols <= 8
    total = n_row * n_col * 2 * BLK

    load = pltpu.make_async_copy(tan_hbm.at[0, 0], tan, tan_sem)
    load.start()

    barrier = pltpu.get_barrier_semaphore()
    greeted = 0
    for d in range(1, n_row):
        other = lax.rem(r + d, n_row)
        for to in (c, nxt, prv):
            pl.semaphore_signal(barrier, inc=1, device_id=(other, to), device_id_type=MESH)
            greeted += 1
    for d in range(1, n_col):
        pl.semaphore_signal(barrier, inc=1, device_id=(r, lax.rem(c + d, n_col)), device_id_type=MESH)
        greeted += 1

    flat = basis_ref[...].astype(F32)
    held = [jnp.concatenate([flat[s:s + 1, WIDE * g:WIDE * (g + 1)] for g in range(OCT)], axis=0) for s in range(2)]
    swapped = jnp.full((OCT, WIDE), id_ref[0] & 1, jnp.int32) == 1
    xs[...] = jnp.concatenate(
        [jnp.where(swapped, held[1], held[0]), jnp.where(swapped, held[0], held[1])], axis=0
    ).astype(BF16)

    pl.semaphore_wait(barrier, greeted)
    basis_out = []
    for d in range(n_row):
        to = lax.rem(r + d, n_row)
        copy = pltpu.make_async_remote_copy(
            src_ref=xs, dst_ref=xr.at[r], send_sem=bs_send.at[d], recv_sem=bs_recv.at[r],
            device_id=(to, nxt), device_id_type=MESH)
        copy.start()
        basis_out.append(copy)

    load.wait()
    stored = tan.shape[0]
    place = cols_ref[...] * tile_rows + rows_ref[...]
    place = jnp.where(iota((1, stored), 1) < count_ref[...], place, -1)

    def dense(first, many, g):
        hot = (iota((many, stored), 0) + first == place).astype(F32).astype(BF16)
        d = jnp.dot(hot, tan[:, 512 * g:512 * (g + 1)], preferred_element_type=F32)
        hi = d.astype(BF16)
        return hi, (d - hi.astype(F32)).astype(BF16)

    if small:
        for g in range(OCT):
            both = dense(0, tile_cols * tile_rows, g)
            for part in range(2):
                for h in range(2):
                    at = ((part * 2 + h) * OCT + g) * tile_rows
                    for j in range(tile_cols):
                        a[at:at + tile_rows, 256 * j:256 * (j + 1)] = (
                            both[part][tile_rows * j:tile_rows * (j + 1), 256 * h:256 * (h + 1)])

    lane_k = over_k(iota((8, WIDE), 1), 8)
    own_lane = lane_k == iota((8, WIDE), 0)
    spread_row = iota((WIDE, 256), 0)
    spread_col = iota((WIDE, 256), 1)
    spread = jnp.logical_and(
        spread_row - K * over_k(spread_row, 8) == spread_col - K * over_k(spread_col, 4),
        spread_col < 4 * K).astype(F32).astype(BF16)
    quarter = over_k(iota((BLK, 256), 1), 5)

    own = iota((128, 128), 0)
    wanted = (own & 15) * 8 + lax.shift_right_logical(own, 4)
    res_rows = jnp.where(iota((128, 128), 1) == wanted, jnp.broadcast_to(res_ref[...], (128, 128)), 0.0)
    at_k = (iota((128, 128), 1) == K).astype(F32).astype(BF16)
    res_col = jnp.zeros((128, 128), F32)
    for piece in reversed(pieces(res_rows)):
        res_col += jnp.dot(piece, at_k, preferred_element_type=F32)
    tile_row = iota((128, WIDE), 0)
    tile_col = iota((128, WIDE), 1)
    tile = (tile_row - SIDE == tile_col - K * over_k(tile_col, 8)).astype(F32).astype(BF16)

    for q in range(n_row):
        pltpu.make_async_remote_copy(
            src_ref=xs, dst_ref=xr.at[q], send_sem=bs_send.at[0], recv_sem=bs_recv.at[q],
            device_id=(r, nxt), device_id_type=MESH).wait_recv()

    for q in range(n_row):
        blocks = xr[q].astype(F32)
        opened = jnp.concatenate(
            [jnp.where(own_lane, jnp.broadcast_to(blocks[s:s + 1], (8, WIDE)), 0.0) for s in range(2 * OCT)],
            axis=0).astype(BF16)
        wide = jnp.dot(opened, spread, preferred_element_type=F32)
        for m in range(2):
            for e in range(4):
                at = (2 * q + m) * 256 + e * BLK
                w[at:at + BLK, :] = jnp.where(quarter == e, wide[BLK * m:BLK * (m + 1)], 0.0).astype(BF16)

    def put(g, left, right):
        turned = pltpu.roll(right, 64, 1)
        row = pl.ds(g, tile_rows, stride=OCT)
        ps[0, row, :] = left[:, 0:128]
        ps[1, row, :] = left[:, 128:256] + turned[:, 0:128]
        ps[2, row, :] = turned[:, 128:256]

    half = OCT * tile_rows
    if small:
        prod = jnp.dot(a[...], w[...], preferred_element_type=F32)
        prod = prod[:2 * half] + prod[2 * half:]
        for g in range(OCT):
            put(g, prod[tile_rows * g:tile_rows * (g + 1)], prod[half + tile_rows * g:half + tile_rows * (g + 1)])
    else:
        for g in range(OCT):
            def add(j, acc, g=g):
                hi, lo = dense(j * tile_rows, tile_rows, g)
                lhs = jnp.concatenate([hi[:, :256], hi[:, 256:], lo[:, :256], lo[:, 256:]], axis=0)
                return acc + jnp.dot(lhs, w[pl.ds(pl.multiple_of(j * 256, 256), 256), :], preferred_element_type=F32)
            acc = lax.fori_loop(0, tile_cols, add, jnp.zeros((4 * tile_rows, 256), F32))
            acc = acc[:2 * tile_rows] + acc[2 * tile_rows:]
            put(g, acc[:tile_rows], acc[tile_rows:])

    mine = 2 * OCT
    prod_out = []
    for d in range(1, n_col):
        to = lax.rem(c + d, n_col)
        copy = pltpu.make_async_remote_copy(
            src_ref=ps.at[:, pl.ds(pl.multiple_of(to * mine, mine), mine)], dst_ref=pr.at[c],
            send_sem=p_send.at[d], recv_sem=p_recv.at[c], device_id=(r, to), device_id_type=MESH)
        copy.start()
        prod_out.append(copy)
    product = ps[:, pl.ds(pl.multiple_of(c * mine, mine), mine), :]
    for d in range(1, n_col):
        source = lax.rem(c + d, n_col)
        pltpu.make_async_remote_copy(
            src_ref=ps.at[:, pl.ds(0, mine)], dst_ref=pr.at[source], send_sem=p_send.at[d], recv_sem=p_recv.at[source],
            device_id=(r, source), device_id_type=MESH).wait_recv()
        product += pr[source]
    product = jnp.concatenate([product[0], product[1], product[2]], axis=1)

    lane = iota((2 * OCT, 128), 1)
    turned = [product if b == 0 else pltpu.roll(product, WIDE - K * b, 1) for b in range(8)]
    stacked = jnp.concatenate([jnp.where(lane < K, t[:, :128], 0.0) for t in turned], axis=0) + res_col
    gram = lax.dot_general(stacked, stacked, (((0,), (0,)), ((), ())), precision=lax.Precision.HIGHEST,
                           preferred_element_type=F32)
    packed = gram[:24] + pltpu.roll(gram[24:48], SIDE, 1)

    ga[r] = packed
    sent = []
    for d in range(1, n_row):
        to = lax.rem(r + d, n_row)
        copy = pltpu.make_async_remote_copy(
            src_ref=ga.at[r], dst_ref=ga.at[r], send_sem=ga_send.at[d], recv_sem=ga_recv.at[r],
            device_id=(to, c), device_id_type=MESH)
        copy.start()
        sent.append(copy)
    for d in range(1, n_row):
        source = lax.rem(r + d, n_row)
        pltpu.make_async_remote_copy(
            src_ref=ga.at[r], dst_ref=ga.at[source], send_sem=ga_send.at[d], recv_sem=ga_recv.at[source],
            device_id=(source, c), device_id_type=MESH).wait_recv()
    packed = ga[0]
    for q in range(1, n_row):
        packed += ga[q]
    gb[c] = packed
    for d in range(1, n_col):
        to = lax.rem(c + d, n_col)
        copy = pltpu.make_async_remote_copy(
            src_ref=gb.at[c], dst_ref=gb.at[c], send_sem=gb_send.at[d], recv_sem=gb_recv.at[c],
            device_id=(r, to), device_id_type=MESH)
        copy.start()
        sent.append(copy)
    for d in range(1, n_col):
        source = lax.rem(c + d, n_col)
        pltpu.make_async_remote_copy(
            src_ref=gb.at[c], dst_ref=gb.at[source], send_sem=gb_send.at[d], recv_sem=gb_recv.at[source],
            device_id=(r, source), device_id_type=MESH).wait_recv()
    packed = gb[0]
    for q in range(1, n_col):
        packed += gb[q]

    row_id = iota((K, 128), 0)
    lane_id = iota((K, 128), 1)
    packed = packed * F32(1.0 / total)
    m = jnp.concatenate([packed, pltpu.roll(packed, SIDE, 1)], axis=0)
    m = jnp.where(lane_id < SIDE, m, (lane_id - SIDE == row_id).astype(F32))
    tiles = [m[8 * t:8 * (t + 1)] for t in range(K // 8)]
    sub = iota((8, 128), 0)
    for j in range(K):
        t0, s0 = j // 8, j % 8
        row = jnp.broadcast_to(tiles[t0][s0:s0 + 1, :], (8, 128))
        inv = 1.0 / jnp.broadcast_to(tiles[t0][s0:s0 + 1, j:j + 1], (8, 128))
        scaled = row * inv
        for t in range(t0, K // 8):
            if t == t0 and s0 == 7:
                continue
            col = jnp.broadcast_to(tiles[t][:, j:j + 1], (8, 128))
            if t == t0:
                col = jnp.where(sub > s0, col, 0.0)
            tiles[t] = tiles[t] - col * scaled
    m = jnp.concatenate(tiles, axis=0)
    pivots = jnp.sum(jnp.where(lane_id == row_id, m, 0.0), axis=1, keepdims=True)
    m = m * lax.rsqrt(jnp.broadcast_to(pivots, (K, 128)))
    coef = jnp.broadcast_to(m[:, K:K + 1], (K, 128)) * F32(math.sqrt(total))
    coef_ref[...] = jnp.sum(jnp.where(lane_id == row_id, coef, 0.0), axis=0, keepdims=True)

    inverse = jnp.where(lane_id >= SIDE, m, 0.0)
    diag_row = over_k(iota((K, WIDE), 1), 8)
    left = jnp.concatenate(list(pieces(product)) + [xr[r]], axis=0)
    acc = [None, None]
    for n, piece in enumerate(pieces(inverse)):
        wide = jnp.dot(piece, tile, preferred_element_type=F32)
        big = jnp.concatenate([jnp.where(diag_row == b, wide, 0.0) for b in range(8)], axis=0).astype(BF16)
        out = lax.dot_general(left, big, (((1,), (1,)), ((), ())), preferred_element_type=F32)
        c_part = out[0:mine]
        for extra in range(1, 3 - n):
            c_part = c_part + out[extra * mine:(extra + 1) * mine]
        u_part = out[3 * mine:4 * mine]
        acc = [c_part, u_part] if n == 0 else [acc[0] + c_part, acc[1] + u_part]
    c_ref[...] = acc[0].astype(BF16)
    u_ref[...] = acc[1].astype(BF16)

    for copy in basis_out + prod_out + sent:
        copy.wait_send()


def per_device(n_row, n_col, tangent, block_row, block_col, tile_count, old_basis, old_id, residual):
    stored = tangent.shape[2]
    tile_rows = 2 * n_col
    tile_cols = 2 * n_row
    small = tile_cols <= 8
    vmem = pl.BlockSpec(memory_space=pltpu.VMEM)
    dma = pltpu.SemaphoreType.DMA
    c16, u16, coef = pl.pallas_call(
        functools.partial(kernel, n_row, n_col, tile_rows, tile_cols),
        out_shape=(
            jax.ShapeDtypeStruct((2 * OCT, WIDE), BF16),
            jax.ShapeDtypeStruct((2 * OCT, WIDE), BF16),
            jax.ShapeDtypeStruct((1, 128), F32),
        ),
        in_specs=[pl.BlockSpec(memory_space=pl.ANY), vmem, vmem, vmem, vmem,
                  pl.BlockSpec(memory_space=pltpu.SMEM), vmem],
        out_specs=(vmem, vmem, vmem),
        scratch_shapes=[
            pltpu.VMEM((stored, BLK * BLK), BF16),
            pltpu.VMEM((2 * OCT, WIDE), BF16),
            pltpu.VMEM((n_row, 2 * OCT, WIDE), BF16),
            pltpu.VMEM((tile_cols * 256, 256), BF16),
            pltpu.VMEM((4 * OCT * tile_rows, tile_cols * 256) if small else (16, 128), BF16),
            pltpu.VMEM((3, OCT * tile_rows, 128), F32),
            pltpu.VMEM((n_col, 3, 2 * OCT, 128), F32),
            pltpu.VMEM((n_row, 24, 128), F32),
            pltpu.VMEM((n_col, 24, 128), F32),
            dma, dma((n_row,)), dma((n_row,)), dma((n_col,)), dma((n_col,)),
            dma((n_row,)), dma((n_row,)), dma((n_col,)), dma((n_col,)),
        ],
        compiler_params=pltpu.CompilerParams(
            collective_id=0, has_side_effects=True, vmem_limit_bytes=40 * 1024 * 1024),
        name="refresh",
    )(tangent, block_row.reshape(1, stored), block_col.reshape(1, stored), tile_count.reshape(1, 1),
      old_basis, old_id, residual.reshape(1, 2 * BLK))
    return c16.reshape(2, BLK * K), u16.reshape(2, BLK * K), coef[0, :K]


def solution(mesh):
    return jax.shard_map(
        functools.partial(per_device, mesh.shape["row"], mesh.shape["col"]),
        mesh=mesh,
        in_specs=(
            P("row", "col", None, None),
            P("row", "col", None),
            P("row", "col", None),
            P("row", "col"),
            P(("row", "col"), None),
            P(("row", "col")),
            P(("row", "col")),
        ),
        out_specs=(P(("row", "col"), None), P(("row", "col"), None), P()),
        check_vma=False,
    )
```

```python
import functools
import math

import jax
import jax.numpy as jnp
from jax import lax
from jax.experimental import pallas as pl
from jax.experimental.pallas import tpu as pltpu
from jax.sharding import PartitionSpec as P

BLK = 64
K = 48
OCT = BLK // 8
WIDE = 8 * K
SIDE = 64
MESH = pl.DeviceIdType.MESH
F32 = jnp.float32
BF16 = jnp.bfloat16


def iota(shape, dim):
    return lax.broadcasted_iota(jnp.int32, shape, dim)


def over_k(index, most):
    whole = jnp.zeros_like(index)
    for step in range(1, most):
        whole += (index >= K * step).astype(jnp.int32)
    return whole


def pieces(x):
    hi = x.astype(BF16)
    rest = x - hi.astype(F32)
    mid = rest.astype(BF16)
    lo = (rest - mid.astype(F32)).astype(BF16)
    return hi, mid, lo


def kernel(n_row, n_col, tile_rows, tile_cols, tan_hbm, rows_hbm, cols_hbm, count_hbm, basis_hbm, id_hbm,
           res_hbm, product_ref, own_ref, gram_ref,
           tan, rows_ref, cols_ref, count_ref, basis_ref, id_ref, res_ref, xs, xr, w, a, ps, pr, ga, gb,
           load_sem, bs_send, bs_recv, p_send, p_recv, ga_send, ga_recv, gb_send, gb_recv):
    r = lax.axis_index("row")
    c = lax.axis_index("col")
    nxt = lax.rem(c + 1, n_col)
    prv = lax.rem(c + n_col - 1, n_col)
    small = tile_cols <= 8
    total = n_row * n_col * 2 * BLK

    loads = [pltpu.make_async_copy(src, dst, load_sem.at[n]) for n, (src, dst) in enumerate((
        (basis_hbm, basis_ref), (id_hbm, id_ref), (tan_hbm.at[0, 0], tan), (rows_hbm, rows_ref),
        (cols_hbm, cols_ref), (count_hbm, count_ref), (res_hbm, res_ref)))]
    for load in loads:
        load.start()

    barrier = pltpu.get_barrier_semaphore()
    greeted = 0
    for d in range(1, n_row):
        other = lax.rem(r + d, n_row)
        for to in (c, nxt, prv):
            pl.semaphore_signal(barrier, inc=1, device_id=(other, to), device_id_type=MESH)
            greeted += 1
    for d in range(1, n_col):
        pl.semaphore_signal(barrier, inc=1, device_id=(r, lax.rem(c + d, n_col)), device_id_type=MESH)
        greeted += 1

    loads[0].wait()
    loads[1].wait()
    flat = basis_ref[...].astype(F32)
    held = [jnp.concatenate([flat[s:s + 1, WIDE * g:WIDE * (g + 1)] for g in range(OCT)], axis=0) for s in range(2)]
    swapped = jnp.full((OCT, WIDE), id_ref[0] & 1, jnp.int32) == 1
    xs[...] = jnp.concatenate(
        [jnp.where(swapped, held[1], held[0]), jnp.where(swapped, held[0], held[1])], axis=0
    ).astype(BF16)

    pl.semaphore_wait(barrier, greeted)
    basis_out = []
    for d in range(n_row):
        to = lax.rem(r + d, n_row)
        copy = pltpu.make_async_remote_copy(
            src_ref=xs, dst_ref=xr.at[r], send_sem=bs_send.at[d], recv_sem=bs_recv.at[r],
            device_id=(to, nxt), device_id_type=MESH)
        copy.start()
        basis_out.append(copy)

    for load in loads[2:]:
        load.wait()
    stored = tan.shape[0]
    place = cols_ref[0] * tile_rows + rows_ref[0]
    place = jnp.where(iota((1, stored), 1) < count_ref[0, 0], place, -1)

    def live(first, many):
        return (iota((many, stored), 0) + first == place).astype(F32).astype(BF16)

    def dense(hot, g):
        d = jnp.dot(hot, tan[:, 512 * g:512 * (g + 1)], preferred_element_type=F32)
        hi = d.astype(BF16)
        return hi, (d - hi.astype(F32)).astype(BF16)

    if small:
        hot = live(0, tile_cols * tile_rows)
        for g in range(OCT):
            both = dense(hot, g)
            for part in range(2):
                for h in range(2):
                    at = ((part * 2 + h) * OCT + g) * tile_rows
                    for j in range(tile_cols):
                        a[at:at + tile_rows, 256 * j:256 * (j + 1)] = (
                            both[part][tile_rows * j:tile_rows * (j + 1), 256 * h:256 * (h + 1)])

    lane_k = over_k(iota((8, WIDE), 1), 8)
    own_lane = lane_k == iota((8, WIDE), 0)
    spread_row = iota((WIDE, 256), 0)
    spread_col = iota((WIDE, 256), 1)
    spread = jnp.logical_and(
        spread_row - K * over_k(spread_row, 8) == spread_col - K * over_k(spread_col, 4),
        spread_col < 4 * K).astype(F32).astype(BF16)
    quarter = over_k(iota((BLK, 256), 1), 5)

    own = iota((128, 128), 0)
    wanted = (own & 15) * 8 + lax.shift_right_logical(own, 4)
    res_rows = jnp.where(iota((128, 128), 1) == wanted, jnp.broadcast_to(res_ref[...].reshape(1, 128), (128, 128)), 0.0)
    at_k = (iota((128, 128), 1) == K).astype(F32).astype(BF16)
    res_col = jnp.zeros((128, 128), F32)
    for piece in reversed(pieces(res_rows)):
        res_col += jnp.dot(piece, at_k, preferred_element_type=F32)
    for q in range(n_row):
        pltpu.make_async_remote_copy(
            src_ref=xs, dst_ref=xr.at[q], send_sem=bs_send.at[0], recv_sem=bs_recv.at[q],
            device_id=(r, nxt), device_id_type=MESH).wait_recv()

    for q in range(n_row):
        blocks = xr[q].astype(F32)
        opened = jnp.concatenate(
            [jnp.where(own_lane, jnp.broadcast_to(blocks[s:s + 1], (8, WIDE)), 0.0) for s in range(2 * OCT)],
            axis=0).astype(BF16)
        wide = jnp.dot(opened, spread, preferred_element_type=F32)
        for m in range(2):
            for e in range(4):
                at = (2 * q + m) * 256 + e * BLK
                w[at:at + BLK, :] = jnp.where(quarter == e, wide[BLK * m:BLK * (m + 1)], 0.0).astype(BF16)

    def put(g, left, right):
        turned = pltpu.roll(right, 64, 1)
        row = pl.ds(g, tile_rows, stride=OCT)
        ps[0, row, :] = left[:, 0:128]
        ps[1, row, :] = left[:, 128:256] + turned[:, 0:128]
        ps[2, row, :] = turned[:, 128:256]

    half = OCT * tile_rows
    if small:
        prod = jnp.dot(a[...], w[...], preferred_element_type=F32)
        prod = prod[:2 * half] + prod[2 * half:]
        for g in range(OCT):
            put(g, prod[tile_rows * g:tile_rows * (g + 1)], prod[half + tile_rows * g:half + tile_rows * (g + 1)])
    else:
        for g in range(OCT):
            def add(j, acc, g=g):
                hi, lo = dense(live(j * tile_rows, tile_rows), g)
                lhs = jnp.concatenate([hi[:, :256], hi[:, 256:], lo[:, :256], lo[:, 256:]], axis=0)
                return acc + jnp.dot(lhs, w[pl.ds(pl.multiple_of(j * 256, 256), 256), :], preferred_element_type=F32)
            acc = lax.fori_loop(0, tile_cols, add, jnp.zeros((4 * tile_rows, 256), F32))
            acc = acc[:2 * tile_rows] + acc[2 * tile_rows:]
            put(g, acc[:tile_rows], acc[tile_rows:])

    mine = 2 * OCT
    prod_out = []
    for d in range(1, n_col):
        to = lax.rem(c + d, n_col)
        copy = pltpu.make_async_remote_copy(
            src_ref=ps.at[:, pl.ds(pl.multiple_of(to * mine, mine), mine)], dst_ref=pr.at[c],
            send_sem=p_send.at[d], recv_sem=p_recv.at[c], device_id=(r, to), device_id_type=MESH)
        copy.start()
        prod_out.append(copy)
    product = ps[:, pl.ds(pl.multiple_of(c * mine, mine), mine), :]
    for d in range(1, n_col):
        source = lax.rem(c + d, n_col)
        pltpu.make_async_remote_copy(
            src_ref=ps.at[:, pl.ds(0, mine)], dst_ref=pr.at[source], send_sem=p_send.at[d], recv_sem=p_recv.at[source],
            device_id=(r, source), device_id_type=MESH).wait_recv()
        product += pr[source]
    product = jnp.concatenate([product[0], product[1], product[2]], axis=1)

    lane = iota((2 * OCT, 128), 1)
    turned = [product if b == 0 else pltpu.roll(product, WIDE - K * b, 1) for b in range(8)]
    stacked = jnp.concatenate([jnp.where(lane < K, t[:, :128], 0.0) for t in turned], axis=0) + res_col
    gram = lax.dot_general(stacked, stacked, (((0,), (0,)), ((), ())), precision=lax.Precision.HIGHEST,
                           preferred_element_type=F32)
    packed = gram[:24] + pltpu.roll(gram[24:48], SIDE, 1)

    pair, side = c // 2, lax.rem(c, 2)
    place_a = r * 2 + side
    ga[place_a] = packed
    sent = []
    others = []
    for d in range(2 * n_row):
        if d:
            row_to = lax.rem(r + d // 2, n_row)
            side_to = lax.rem(side + d % 2, 2)
            others.append((row_to * 2 + side_to, row_to, pair * 2 + side_to))
    for d, (slot, row_to, col_to) in enumerate(others):
        copy = pltpu.make_async_remote_copy(
            src_ref=ga.at[place_a], dst_ref=ga.at[place_a], send_sem=ga_send.at[d], recv_sem=ga_recv.at[place_a],
            device_id=(row_to, col_to), device_id_type=MESH)
        copy.start()
        sent.append(copy)
    for d, (slot, row_to, col_to) in enumerate(others):
        pltpu.make_async_remote_copy(
            src_ref=ga.at[place_a], dst_ref=ga.at[slot], send_sem=ga_send.at[d], recv_sem=ga_recv.at[slot],
            device_id=(row_to, col_to), device_id_type=MESH).wait_recv()
    packed = ga[0]
    for q in range(1, 2 * n_row):
        packed += ga[q]
    gb[pair] = packed
    pairs = n_col // 2
    for d in range(1, pairs):
        to = lax.rem(pair + d, pairs) * 2 + side
        copy = pltpu.make_async_remote_copy(
            src_ref=gb.at[pair], dst_ref=gb.at[pair], send_sem=gb_send.at[d], recv_sem=gb_recv.at[pair],
            device_id=(r, to), device_id_type=MESH)
        copy.start()
        sent.append(copy)
    product_ref[...] = product
    own_ref[...] = xr[r]
    for d in range(1, pairs):
        source = lax.rem(pair + d, pairs)
        pltpu.make_async_remote_copy(
            src_ref=gb.at[pair], dst_ref=gb.at[source], send_sem=gb_send.at[d], recv_sem=gb_recv.at[source],
            device_id=(r, source * 2 + side), device_id_type=MESH).wait_recv()
    packed = gb[0]
    for q in range(1, pairs):
        packed += gb[q]
    gram_ref[...] = packed

    for copy in basis_out + prod_out + sent:
        copy.wait_send()


def eliminate(tiles):
    sub = iota((8, 128), 0)
    done = []
    for t0 in range(K // 8):
        j = 8 * t0
        cols = [[jnp.broadcast_to(tiles[t][:, j + k:j + k + 1], (8, 128)) for t in range(t0, K // 8)] for k in range(8)]
        rows = [jnp.broadcast_to(tiles[t0][i:i + 1, :], (8, 128)) for i in range(8)]
        s = [[jnp.broadcast_to(cols[k][0][i:i + 1, :], (8, 128)) if i >= k else None for k in range(8)] for i in range(8)]
        inv = []
        scale = jnp.zeros((8, 128), F32)
        for k in range(8):
            inv.append(1.0 / s[k][k])
            scale = jnp.where(sub == k, lax.rsqrt(s[k][k]), scale)
            for i in range(k + 1, 8):
                low = s[i][k] * inv[k]
                rows[i] = rows[i] - low * rows[k]
                for n in range(1, K // 8 - t0):
                    cols[i][n] = cols[i][n] - cols[k][n] * low
                for i2 in range(i, 8):
                    s[i2][i] = s[i2][i] - s[i2][k] * low
        for n in range(1, K // 8 - t0):
            gone = cols[0][n] * (rows[0] * inv[0])
            for k in range(1, 8):
                gone = gone + cols[k][n] * (rows[k] * inv[k])
            tiles[t0 + n] = tiles[t0 + n] - gone
        mixed = rows[0]
        for k in range(1, 8):
            mixed = jnp.where(sub == k, rows[k], mixed)
        done.append(mixed * scale)
    return jnp.concatenate(done, axis=0)


def finish(total, product_ref, own_ref, gram_ref, c_ref, u_ref, coef_ref):
    row_id = iota((K, 128), 0)
    lane_id = iota((K, 128), 1)
    packed = gram_ref[...] * F32(1.0 / total)
    m = jnp.concatenate([packed, pltpu.roll(packed, SIDE, 1)], axis=0)
    m = jnp.where(lane_id < SIDE, m, (lane_id - SIDE == row_id).astype(F32))
    m = eliminate([m[8 * t:8 * (t + 1)] for t in range(K // 8)])
    coef = jnp.broadcast_to(m[:, K:K + 1], (K, 128)) * F32(math.sqrt(total))
    coef_ref[...] = jnp.sum(jnp.where(lane_id == row_id, coef, 0.0), axis=0, keepdims=True)[:, :K]

    tile_row = iota((128, WIDE), 0)
    tile_col = iota((128, WIDE), 1)
    tile = (tile_row - SIDE == tile_col - K * over_k(tile_col, 8)).astype(F32).astype(BF16)
    mine = 2 * OCT
    inverse = jnp.where(lane_id >= SIDE, m, 0.0)
    diag_row = over_k(iota((K, WIDE), 1), 8)
    left = jnp.concatenate(list(pieces(product_ref[...])) + [own_ref[...]], axis=0)
    acc = [None, None]
    for n, piece in enumerate(pieces(inverse)):
        wide = jnp.dot(piece, tile, preferred_element_type=F32)
        big = jnp.concatenate([jnp.where(diag_row == b, wide, 0.0) for b in range(8)], axis=0).astype(BF16)
        out = lax.dot_general(left, big, (((1,), (1,)), ((), ())), preferred_element_type=F32)
        c_part = out[0:mine]
        for extra in range(1, 3 - n):
            c_part = c_part + out[extra * mine:(extra + 1) * mine]
        u_part = out[3 * mine:4 * mine]
        acc = [c_part, u_part] if n == 0 else [acc[0] + c_part, acc[1] + u_part]
    for ref, whole in ((c_ref, acc[0]), (u_ref, acc[1])):
        ref[...] = jnp.concatenate(
            [jnp.concatenate([whole[g:g + 1], whole[OCT + g:OCT + g + 1]], axis=0) for g in range(OCT)], axis=1
        ).astype(BF16)


def per_device(n_row, n_col, tangent, block_row, block_col, tile_count, old_basis, old_id, residual):
    stored = tangent.shape[2]
    tile_rows = 2 * n_col
    tile_cols = 2 * n_row
    small = tile_cols <= 8
    vmem = pl.BlockSpec(memory_space=pltpu.VMEM)
    dma = pltpu.SemaphoreType.DMA
    product, own, gram = pl.pallas_call(
        functools.partial(kernel, n_row, n_col, tile_rows, tile_cols),
        out_shape=(
            jax.ShapeDtypeStruct((2 * OCT, WIDE), F32),
            jax.ShapeDtypeStruct((2 * OCT, WIDE), BF16),
            jax.ShapeDtypeStruct((24, 128), F32),
        ),
        in_specs=[pl.BlockSpec(memory_space=pltpu.HBM)] * 7,
        out_specs=(vmem, vmem, vmem),
        scratch_shapes=[
            pltpu.VMEM((stored, BLK * BLK), BF16),
            pltpu.VMEM((1, 1, stored), jnp.int32),
            pltpu.VMEM((1, 1, stored), jnp.int32),
            pltpu.SMEM((1, 1), jnp.int32),
            pltpu.VMEM((2, BLK * K), BF16),
            pltpu.SMEM((2,), jnp.int32),
            pltpu.VMEM((2 * BLK,), F32),
            pltpu.VMEM((2 * OCT, WIDE), BF16),
            pltpu.VMEM((n_row, 2 * OCT, WIDE), BF16),
            pltpu.VMEM((tile_cols * 256, 256), BF16),
            pltpu.VMEM((4 * OCT * tile_rows, tile_cols * 256) if small else (16, 128), BF16),
            pltpu.VMEM((3, OCT * tile_rows, 128), F32),
            pltpu.VMEM((n_col, 3, 2 * OCT, 128), F32),
            pltpu.VMEM((2 * n_row, 24, 128), F32),
            pltpu.VMEM((n_col // 2, 24, 128), F32),
            dma((7,)), dma((n_row,)), dma((n_row,)), dma((n_col,)), dma((n_col,)),
            dma((2 * n_row,)), dma((2 * n_row,)), dma((n_col // 2,)), dma((n_col // 2,)),
        ],
        compiler_params=pltpu.CompilerParams(
            collective_id=0, has_side_effects=True, vmem_limit_bytes=64 * 1024 * 1024),
        name="reduce",
    )(tangent, block_row, block_col, tile_count, old_basis, old_id, residual)
    recycled_c, recycled_u, coefficients = pl.pallas_call(
        functools.partial(finish, n_row * n_col * 2 * BLK),
        out_shape=(
            jax.ShapeDtypeStruct((2, BLK * K), BF16),
            jax.ShapeDtypeStruct((2, BLK * K), BF16),
            jax.ShapeDtypeStruct((1, K), F32),
        ),
        in_specs=[vmem] * 3,
        out_specs=(vmem, vmem, vmem),
        compiler_params=pltpu.CompilerParams(vmem_limit_bytes=16 * 1024 * 1024),
        name="finish",
    )(product, own, gram)
    return recycled_c, recycled_u, coefficients[0]


def solution(mesh):
    return jax.shard_map(
        functools.partial(per_device, mesh.shape["row"], mesh.shape["col"]),
        mesh=mesh,
        in_specs=(
            P("row", "col", None, None),
            P("row", "col", None),
            P("row", "col", None),
            P("row", "col"),
            P(("row", "col"), None),
            P(("row", "col")),
            P(("row", "col")),
        ),
        out_specs=(P(("row", "col"), None), P(("row", "col"), None), P()),
        check_vma=False,
    )
```

```python
import functools
import math

import jax
import jax.numpy as jnp
from jax import lax
from jax.experimental import pallas as pl
from jax.experimental.pallas import tpu as pltpu
from jax.sharding import PartitionSpec as P

BLK = 64
K = 48
OCT = BLK // 8
WIDE = 8 * K
SIDE = 64
MESH = pl.DeviceIdType.MESH
F32 = jnp.float32
BF16 = jnp.bfloat16


def iota(shape, dim):
    return lax.broadcasted_iota(jnp.int32, shape, dim)


def over_k(index, most):
    whole = jnp.zeros_like(index)
    for step in range(1, most):
        whole += (index >= K * step).astype(jnp.int32)
    return whole


def pieces(x):
    hi = x.astype(BF16)
    rest = x - hi.astype(F32)
    mid = rest.astype(BF16)
    lo = (rest - mid.astype(F32)).astype(BF16)
    return hi, mid, lo


def kernel(n_row, n_col, tile_rows, tile_cols, tan_hbm, rows_hbm, cols_hbm, count_hbm, basis_hbm, id_hbm,
           res_hbm, out_ref,
           tan, rows_ref, cols_ref, count_ref, basis_ref, id_ref, res_ref, xs, xr, w, a, ps, pr, ga, gb,
           load_sem, bs_send, bs_recv, p_send, p_recv, ga_send, ga_recv, gb_send, gb_recv):
    r = lax.axis_index("row")
    c = lax.axis_index("col")
    nxt = lax.rem(c + 1, n_col)
    prv = lax.rem(c + n_col - 1, n_col)
    small = tile_cols <= 8 and tile_rows == 16
    lead = n_col // 4

    loads = [pltpu.make_async_copy(src, dst, load_sem.at[n]) for n, (src, dst) in enumerate((
        (basis_hbm, basis_ref), (id_hbm, id_ref), (tan_hbm.at[0, 0], tan), (rows_hbm, rows_ref),
        (cols_hbm, cols_ref), (count_hbm, count_ref), (res_hbm, res_ref)))]
    for load in loads:
        load.start()

    barrier = pltpu.get_barrier_semaphore()
    greeted = 0
    for d in range(1, n_row):
        other = lax.rem(r + d, n_row)
        for to in (c, nxt, prv):
            pl.semaphore_signal(barrier, inc=1, device_id=(other, to), device_id_type=MESH)
            greeted += 1
    for d in range(1, n_col):
        pl.semaphore_signal(barrier, inc=1, device_id=(r, lax.rem(c + d, n_col)), device_id_type=MESH)
        greeted += 1

    loads[0].wait()
    loads[1].wait()
    flat = basis_ref[...].astype(F32)
    held = [jnp.concatenate([flat[s:s + 1, WIDE * g:WIDE * (g + 1)] for g in range(OCT)], axis=0) for s in range(2)]
    swapped = jnp.full((OCT, WIDE), id_ref[0] & 1, jnp.int32) == 1
    xs[...] = jnp.concatenate(
        [jnp.where(swapped, held[1], held[0]), jnp.where(swapped, held[0], held[1])], axis=0
    ).astype(BF16)

    pl.semaphore_wait(barrier, greeted)
    basis_out = []
    for d in range(n_row):
        to = lax.rem(r + d, n_row)
        copy = pltpu.make_async_remote_copy(
            src_ref=xs, dst_ref=xr.at[r], send_sem=bs_send.at[d], recv_sem=bs_recv.at[r],
            device_id=(to, nxt), device_id_type=MESH)
        copy.start()
        basis_out.append(copy)

    for load in loads[2:]:
        load.wait()
    stored = tan.shape[0]
    turned_row = rows_ref[0] - 2 * lax.rem(c + lead, n_col)
    place = cols_ref[0] * tile_rows + jnp.where(turned_row < 0, turned_row + tile_rows, turned_row)
    place = jnp.where(iota((1, stored), 1) < count_ref[0, 0], place, -1)

    def live(first, many):
        return (iota((many, stored), 0) + first == place).astype(F32).astype(BF16)

    def dense(hot, g):
        d = jnp.dot(hot, tan[:, 512 * g:512 * (g + 1)], preferred_element_type=F32)
        hi = d.astype(BF16).astype(F32)
        return hi, d - hi

    if small:
        hot = live(0, tile_cols * tile_rows)
        for g in range(OCT):
            hi, lo = dense(hot, g)
            for half in range(2):
                for h in range(2):
                    at = ((half * 2 + h) * OCT + g) * 16
                    for j in range(tile_cols):
                        take = (slice(16 * j + 8 * half, 16 * j + 8 * half + 8), slice(256 * h, 256 * (h + 1)))
                        a[at:at + 16, 256 * j:256 * (j + 1)] = jnp.concatenate([hi[take], lo[take]], axis=0).astype(BF16)

    lane_k = over_k(iota((8, WIDE), 1), 8)
    own_lane = lane_k == iota((8, WIDE), 0)
    spread_row = iota((WIDE, 256), 0)
    spread_col = iota((WIDE, 256), 1)
    spread = jnp.logical_and(
        spread_row - K * over_k(spread_row, 8) == spread_col - K * over_k(spread_col, 4),
        spread_col < 4 * K).astype(F32).astype(BF16)
    quarter = over_k(iota((BLK, 256), 1), 5)

    for q in range(n_row):
        pltpu.make_async_remote_copy(
            src_ref=xs, dst_ref=xr.at[q], send_sem=bs_send.at[0], recv_sem=bs_recv.at[q],
            device_id=(r, nxt), device_id_type=MESH).wait_recv()

    for q in range(n_row):
        blocks = xr[q].astype(F32)
        opened = jnp.concatenate(
            [jnp.where(own_lane, jnp.broadcast_to(blocks[s:s + 1], (8, WIDE)), 0.0) for s in range(2 * OCT)],
            axis=0).astype(BF16)
        wide = jnp.dot(opened, spread, preferred_element_type=F32)
        for m in range(2):
            for e in range(4):
                at = (2 * q + m) * 256 + e * BLK
                w[at:at + BLK, :] = jnp.where(quarter == e, wide[BLK * m:BLK * (m + 1)], 0.0).astype(BF16)

    def put(first, g, left, right):
        turned = pltpu.roll(right, 64, 1)
        row = pl.ds(first * OCT + g, left.shape[0], stride=OCT)
        ps[0, row, :] = left[:, 0:128]
        ps[1, row, :] = left[:, 128:256] + turned[:, 0:128]
        ps[2, row, :] = turned[:, 128:256]

    mine = 2 * OCT
    prod_out = []

    def send(places):
        for p in sorted(places, key=lambda p: abs((p + lead) % n_col * 2 - n_col)):
            d = (p + lead) % n_col
            if d:
                copy = pltpu.make_async_remote_copy(
                    src_ref=ps.at[:, pl.ds(p * mine, mine)], dst_ref=pr.at[c],
                    send_sem=p_send.at[d], recv_sem=p_recv.at[c], device_id=(r, lax.rem(c + d, n_col)),
                    device_id_type=MESH)
                copy.start()
                prod_out.append(copy)

    if small:
        for half in range(2):
            prod = jnp.dot(a[256 * half:256 * (half + 1), :], w[...], preferred_element_type=F32)
            slabs = [prod[16 * n:16 * n + 8] + prod[16 * n + 8:16 * n + 16] for n in range(2 * OCT)]
            for g in range(OCT):
                put(8 * half, g, slabs[g], slabs[OCT + g])
            send(range(4 * half, 4 * half + 4))
    else:
        for g in range(OCT):
            def add(j, acc, g=g):
                hi, lo = dense(live(j * tile_rows, tile_rows), g)
                lhs = jnp.concatenate([hi[:, :256], hi[:, 256:], lo[:, :256], lo[:, 256:]], axis=0).astype(BF16)
                return acc + jnp.dot(lhs, w[pl.ds(pl.multiple_of(j * 256, 256), 256), :], preferred_element_type=F32)
            acc = lax.fori_loop(0, tile_cols, add, jnp.zeros((4 * tile_rows, 256), F32))
            acc = acc[:2 * tile_rows] + acc[2 * tile_rows:]
            put(0, g, acc[:tile_rows], acc[tile_rows:])
        send(range(n_col))

    own = iota((128, 128), 0)
    wanted = (own & 15) * 8 + lax.shift_right_logical(own, 4)
    res_rows = jnp.where(iota((128, 128), 1) == wanted, jnp.broadcast_to(res_ref[...].reshape(1, 128), (128, 128)), 0.0)
    at_k = (iota((128, 128), 1) == K).astype(F32).astype(BF16)
    res_col = jnp.zeros((128, 128), F32)
    for piece in reversed(pieces(res_rows)):
        res_col += jnp.dot(piece, at_k, preferred_element_type=F32)
    product = ps[:, (n_col - lead) * mine:(n_col - lead + 1) * mine, :]
    for d in range(1, n_col):
        source = lax.rem(c + d, n_col)
        pltpu.make_async_remote_copy(
            src_ref=ps.at[:, pl.ds(0, mine)], dst_ref=pr.at[source], send_sem=p_send.at[d], recv_sem=p_recv.at[source],
            device_id=(r, source), device_id_type=MESH).wait_recv()
        product += pr[source]
    product = jnp.concatenate([product[0], product[1], product[2]], axis=1)

    lane = iota((2 * OCT, 128), 1)
    turned = [product if b == 0 else pltpu.roll(product, WIDE - K * b, 1) for b in range(8)]
    stacked = jnp.concatenate([jnp.where(lane < K, t[:, :128], 0.0) for t in turned], axis=0) + res_col
    gram = lax.dot_general(stacked, stacked, (((0,), (0,)), ((), ())), precision=lax.Precision.HIGHEST,
                           preferred_element_type=F32)
    parts = [gram[16 * n:16 * (n + 1)] for n in range(3)]
    packed = parts[0]
    for first, n, by in ((16, 1, 16), (48, 2, 48), (96, 0, 48), (97, 1, 49), (98, 2, 50)):
        packed = jnp.where(lane >= first, pltpu.roll(parts[n], by, 1), packed)

    pair, side = c // 2, lax.rem(c, 2)
    place_a = r * 2 + side
    ga[place_a] = packed
    sent = []
    others = []
    for d in range(2 * n_row):
        if d:
            row_to = lax.rem(r + d // 2, n_row)
            side_to = lax.rem(side + d % 2, 2)
            others.append((row_to * 2 + side_to, row_to, pair * 2 + side_to))
    for d, (slot, row_to, col_to) in enumerate(others):
        copy = pltpu.make_async_remote_copy(
            src_ref=ga.at[place_a], dst_ref=ga.at[place_a], send_sem=ga_send.at[d], recv_sem=ga_recv.at[place_a],
            device_id=(row_to, col_to), device_id_type=MESH)
        copy.start()
        sent.append(copy)
    for d, (slot, row_to, col_to) in enumerate(others):
        pltpu.make_async_remote_copy(
            src_ref=ga.at[place_a], dst_ref=ga.at[slot], send_sem=ga_send.at[d], recv_sem=ga_recv.at[slot],
            device_id=(row_to, col_to), device_id_type=MESH).wait_recv()
    packed = ga[0]
    for q in range(1, 2 * n_row):
        packed += ga[q]
    gb[pair] = packed
    pairs = n_col // 2
    for d in range(1, pairs):
        to = lax.rem(pair + d, pairs) * 2 + side
        copy = pltpu.make_async_remote_copy(
            src_ref=gb.at[pair], dst_ref=gb.at[pair], send_sem=gb_send.at[d], recv_sem=gb_recv.at[pair],
            device_id=(r, to), device_id_type=MESH)
        copy.start()
        sent.append(copy)
    own = xr[r].astype(F32)
    for t in range(3):
        out_ref[16 * t:16 * (t + 1), :] = product[:, 128 * t:128 * (t + 1)]
        out_ref[48 + 16 * t:64 + 16 * t, :] = own[:, 128 * t:128 * (t + 1)]
    for d in range(1, pairs):
        source = lax.rem(pair + d, pairs)
        pltpu.make_async_remote_copy(
            src_ref=gb.at[pair], dst_ref=gb.at[source], send_sem=gb_send.at[d], recv_sem=gb_recv.at[source],
            device_id=(r, source * 2 + side), device_id_type=MESH).wait_recv()
    packed = gb[0]
    for q in range(1, pairs):
        packed += gb[q]
    out_ref[96:112, :] = packed

    for copy in basis_out + prod_out + sent:
        copy.wait_send()


def eliminate(tiles):
    sub = iota((8, 128), 0)
    done = []
    for t0 in range(K // 8):
        j = 8 * t0
        cols = [[jnp.broadcast_to(tiles[t][:, j + k:j + k + 1], (8, 128)) for t in range(t0, K // 8)] for k in range(8)]
        rows = [jnp.broadcast_to(tiles[t0][i:i + 1, :], (8, 128)) for i in range(8)]
        s = [[jnp.broadcast_to(cols[k][0][i:i + 1, :], (8, 128)) if i >= k else None for k in range(8)] for i in range(8)]
        inv = []
        scale = jnp.zeros((8, 128), F32)
        for k in range(8):
            inv.append(1.0 / s[k][k])
            scale = jnp.where(sub == k, lax.rsqrt(s[k][k]), scale)
            for i in range(k + 1, 8):
                low = s[i][k] * inv[k]
                rows[i] = rows[i] - low * rows[k]
                for n in range(1, K // 8 - t0):
                    cols[i][n] = cols[i][n] - cols[k][n] * low
                for i2 in range(i, 8):
                    s[i2][i] = s[i2][i] - s[i2][k] * low
        for n in range(1, K // 8 - t0):
            gone = cols[0][n] * (rows[0] * inv[0])
            for k in range(1, 8):
                gone = gone + cols[k][n] * (rows[k] * inv[k])
            tiles[t0 + n] = tiles[t0 + n] - gone
        mixed = rows[0]
        for k in range(1, 8):
            mixed = jnp.where(sub == k, rows[k], mixed)
        done.append(mixed * scale)
    return jnp.concatenate(done, axis=0)


def finish(total, in_ref, c_ref, u_ref, coef_ref):
    row_id = iota((K, 128), 0)
    lane_id = iota((K, 128), 1)
    packed = in_ref[96:112, :] * F32(1.0 / total)
    low = jnp.concatenate([packed if by == 0 else pltpu.roll(packed, 128 - by, 1) for by in (0, 16, 48)], axis=0)
    beside = jnp.concatenate([pltpu.roll(packed, 128 - by, 1) for by in (48, 49, 50)], axis=0)
    high = jnp.concatenate([low, jnp.zeros((128 - K, 128), F32)], axis=0).T[:K]
    m = jnp.where(lane_id <= (row_id | 15), low, high)
    m = jnp.where(lane_id == K, beside, m)
    m = jnp.where(lane_id < SIDE, m, (lane_id - SIDE == row_id).astype(F32))
    m = eliminate([m[8 * t:8 * (t + 1)] for t in range(K // 8)])
    coef = jnp.broadcast_to(m[:, K:K + 1], (K, 128)) * F32(math.sqrt(total))
    coef_ref[...] = jnp.sum(jnp.where(lane_id == row_id, coef, 0.0), axis=0, keepdims=True)[:, :K]

    tile_row = iota((128, WIDE), 0)
    tile_col = iota((128, WIDE), 1)
    tile = (tile_row - SIDE == tile_col - K * over_k(tile_col, 8)).astype(F32).astype(BF16)
    mine = 2 * OCT
    inverse = jnp.where(lane_id >= SIDE, m, 0.0)
    diag_row = over_k(iota((K, WIDE), 1), 8)
    product, own = (
        jnp.concatenate([in_ref[first + 16 * t:first + 16 * (t + 1), :] for t in range(3)], axis=1) for first in (0, 48))
    left = jnp.concatenate(list(pieces(product)) + [own.astype(BF16)], axis=0)
    acc = [None, None]
    for n, piece in enumerate(pieces(inverse)):
        wide = jnp.dot(piece, tile, preferred_element_type=F32)
        big = jnp.concatenate([jnp.where(diag_row == b, wide, 0.0) for b in range(8)], axis=0).astype(BF16)
        out = lax.dot_general(left, big, (((1,), (1,)), ((), ())), preferred_element_type=F32)
        c_part = out[0:mine]
        for extra in range(1, 3 - n):
            c_part = c_part + out[extra * mine:(extra + 1) * mine]
        u_part = out[3 * mine:4 * mine]
        acc = [c_part, u_part] if n == 0 else [acc[0] + c_part, acc[1] + u_part]
    for ref, whole in ((c_ref, acc[0]), (u_ref, acc[1])):
        ref[...] = jnp.concatenate(
            [jnp.concatenate([whole[g:g + 1], whole[OCT + g:OCT + g + 1]], axis=0) for g in range(OCT)], axis=1
        ).astype(BF16)


def per_device(n_row, n_col, tangent, block_row, block_col, tile_count, old_basis, old_id, residual):
    stored = tangent.shape[2]
    tile_rows = 2 * n_col
    tile_cols = 2 * n_row
    small = tile_cols <= 8 and tile_rows == 16
    vmem = pl.BlockSpec(memory_space=pltpu.VMEM)
    dma = pltpu.SemaphoreType.DMA
    shares = pl.pallas_call(
        functools.partial(kernel, n_row, n_col, tile_rows, tile_cols),
        out_shape=jax.ShapeDtypeStruct((112, 128), F32),
        in_specs=[pl.BlockSpec(memory_space=pltpu.HBM)] * 7,
        out_specs=vmem,
        scratch_shapes=[
            pltpu.VMEM((stored, BLK * BLK), BF16),
            pltpu.VMEM((1, 1, stored), jnp.int32),
            pltpu.VMEM((1, 1, stored), jnp.int32),
            pltpu.SMEM((1, 1), jnp.int32),
            pltpu.VMEM((2, BLK * K), BF16),
            pltpu.SMEM((2,), jnp.int32),
            pltpu.VMEM((2 * BLK,), F32),
            pltpu.VMEM((2 * OCT, WIDE), BF16),
            pltpu.VMEM((n_row, 2 * OCT, WIDE), BF16),
            pltpu.VMEM((tile_cols * 256, 256), BF16),
            pltpu.VMEM((4 * OCT * tile_rows, tile_cols * 256) if small else (16, 128), BF16),
            pltpu.VMEM((3, OCT * tile_rows, 128), F32),
            pltpu.VMEM((n_col, 3, 2 * OCT, 128), F32),
            pltpu.VMEM((2 * n_row, 16, 128), F32),
            pltpu.VMEM((n_col // 2, 16, 128), F32),
            dma((7,)), dma((n_row,)), dma((n_row,)), dma((n_col,)), dma((n_col,)),
            dma((2 * n_row,)), dma((2 * n_row,)), dma((n_col // 2,)), dma((n_col // 2,)),
        ],
        compiler_params=pltpu.CompilerParams(
            collective_id=0, has_side_effects=True, vmem_limit_bytes=64 * 1024 * 1024),
        name="reduce",
    )(tangent, block_row, block_col, tile_count, old_basis, old_id, residual)
    recycled_c, recycled_u, coefficients = pl.pallas_call(
        functools.partial(finish, n_row * n_col * 2 * BLK),
        out_shape=(
            jax.ShapeDtypeStruct((2, BLK * K), BF16),
            jax.ShapeDtypeStruct((2, BLK * K), BF16),
            jax.ShapeDtypeStruct((1, K), F32),
        ),
        in_specs=[vmem],
        out_specs=(vmem, vmem, vmem),
        compiler_params=pltpu.CompilerParams(vmem_limit_bytes=16 * 1024 * 1024),
        name="finish",
    )(shares)
    return recycled_c, recycled_u, coefficients[0]


def solution(mesh):
    return jax.shard_map(
        functools.partial(per_device, mesh.shape["row"], mesh.shape["col"]),
        mesh=mesh,
        in_specs=(
            P("row", "col", None, None),
            P("row", "col", None),
            P("row", "col", None),
            P("row", "col"),
            P(("row", "col"), None),
            P(("row", "col")),
            P(("row", "col")),
        ),
        out_specs=(P(("row", "col"), None), P(("row", "col"), None), P()),
        check_vma=False,
    )
```

```python
import functools
import math

import jax
import jax.numpy as jnp
from jax import lax
from jax.experimental import pallas as pl
from jax.experimental.pallas import tpu as pltpu
from jax.sharding import PartitionSpec as P

BLK = 64
K = 48
OCT = BLK // 8
WIDE = 8 * K
SIDE = 64
MESH = pl.DeviceIdType.MESH
F32 = jnp.float32
BF16 = jnp.bfloat16


def iota(shape, dim):
    return lax.broadcasted_iota(jnp.int32, shape, dim)


def over_k(index, most):
    whole = jnp.zeros_like(index)
    for step in range(1, most):
        whole += (index >= K * step).astype(jnp.int32)
    return whole


def pieces(x):
    hi = x.astype(BF16)
    rest = x - hi.astype(F32)
    mid = rest.astype(BF16)
    lo = (rest - mid.astype(F32)).astype(BF16)
    return hi, mid, lo


def kernel(n_row, n_col, tile_rows, tile_cols, tan_hbm, rows_hbm, cols_hbm, count_hbm, basis_hbm, id_hbm,
           res_hbm, out_ref,
           tan, rows_ref, cols_ref, count_ref, basis_ref, id_ref, res_ref, xs, xr, w, a, ps, pr, ga, gb,
           load_sem, bs_send, bs_recv, p_send, p_recv, ga_send, ga_recv, gb_send, gb_recv):
    r = lax.axis_index("row")
    c = lax.axis_index("col")
    nxt = lax.rem(c + 1, n_col)
    prv = lax.rem(c + n_col - 1, n_col)
    small = tile_cols <= 8 and tile_rows == 16
    lead = n_col // 4

    loads = [pltpu.make_async_copy(src, dst, load_sem.at[n]) for n, (src, dst) in enumerate((
        (basis_hbm, basis_ref), (id_hbm, id_ref), (tan_hbm.at[0, 0], tan), (rows_hbm, rows_ref),
        (cols_hbm, cols_ref), (count_hbm, count_ref), (res_hbm, res_ref)))]
    for load in loads:
        load.start()

    barrier = pltpu.get_barrier_semaphore()
    greeted = 0
    for d in range(1, n_row):
        other = lax.rem(r + d, n_row)
        for to in (c, nxt, prv):
            pl.semaphore_signal(barrier, inc=1, device_id=(other, to), device_id_type=MESH)
            greeted += 1
    for d in range(1, n_col):
        pl.semaphore_signal(barrier, inc=1, device_id=(r, lax.rem(c + d, n_col)), device_id_type=MESH)
        greeted += 1

    lane_k = over_k(iota((8, WIDE), 1), 8)
    own_lane = lane_k == iota((8, WIDE), 0)
    spread_row = iota((WIDE, 256), 0)
    spread_col = iota((WIDE, 256), 1)
    spread = jnp.logical_and(
        spread_row - K * over_k(spread_row, 8) == spread_col - K * over_k(spread_col, 4),
        spread_col < 4 * K).astype(F32).astype(BF16)
    quarter = over_k(iota((BLK, 256), 1), 5)

    loads[0].wait()
    loads[1].wait()
    flat = basis_ref[...].astype(F32)
    held = [jnp.concatenate([flat[s:s + 1, WIDE * g:WIDE * (g + 1)] for g in range(OCT)], axis=0) for s in range(2)]
    swapped = jnp.full((OCT, WIDE), id_ref[0] & 1, jnp.int32) == 1
    xs[...] = jnp.concatenate(
        [jnp.where(swapped, held[1], held[0]), jnp.where(swapped, held[0], held[1])], axis=0
    ).astype(BF16)

    pl.semaphore_wait(barrier, greeted)
    basis_out = []
    for d in range(n_row):
        to = lax.rem(r + d, n_row)
        copy = pltpu.make_async_remote_copy(
            src_ref=xs, dst_ref=xr.at[r], send_sem=bs_send.at[d], recv_sem=bs_recv.at[r],
            device_id=(to, nxt), device_id_type=MESH)
        copy.start()
        basis_out.append(copy)

    for load in loads[2:]:
        load.wait()
    stored = tan.shape[0]
    turned_row = rows_ref[0] - 2 * lax.rem(c + lead, n_col)
    place = cols_ref[0] * tile_rows + jnp.where(turned_row < 0, turned_row + tile_rows, turned_row)
    place = jnp.where(iota((1, stored), 1) < count_ref[0, 0], place, -1)

    def live(first, many):
        return (iota((many, stored), 0) + first == place).astype(F32).astype(BF16)

    def dense(hot, g):
        d = jnp.dot(hot, tan[:, 512 * g:512 * (g + 1)], preferred_element_type=F32)
        hi = d.astype(BF16).astype(F32)
        return hi, d - hi

    if small:
        hot = live(0, tile_cols * tile_rows)
        for g in range(OCT):
            hi, lo = dense(hot, g)
            for half in range(2):
                for h in range(2):
                    at = ((half * 2 + h) * OCT + g) * 16
                    for j in range(tile_cols):
                        take = (slice(16 * j + 8 * half, 16 * j + 8 * half + 8), slice(256 * h, 256 * (h + 1)))
                        a[at:at + 16, 256 * j:256 * (j + 1)] = jnp.concatenate([hi[take], lo[take]], axis=0).astype(BF16)

    for q in range(n_row):
        pltpu.make_async_remote_copy(
            src_ref=xs, dst_ref=xr.at[q], send_sem=bs_send.at[0], recv_sem=bs_recv.at[q],
            device_id=(r, nxt), device_id_type=MESH).wait_recv()

    for q in range(n_row):
        blocks = xr[q].astype(F32)
        opened = jnp.concatenate(
            [jnp.where(own_lane, jnp.broadcast_to(blocks[s:s + 1], (8, WIDE)), 0.0) for s in range(2 * OCT)],
            axis=0).astype(BF16)
        wide = jnp.dot(opened, spread, preferred_element_type=F32)
        for m in range(2):
            for e in range(4):
                at = (2 * q + m) * 256 + e * BLK
                w[at:at + BLK, :] = jnp.where(quarter == e, wide[BLK * m:BLK * (m + 1)], 0.0).astype(BF16)

    def put(first, g, left, right):
        turned = pltpu.roll(right, 64, 1)
        row = pl.ds(first * OCT + g, left.shape[0], stride=OCT)
        ps[0, row, :] = left[:, 0:128]
        ps[1, row, :] = left[:, 128:256] + turned[:, 0:128]
        ps[2, row, :] = turned[:, 128:256]

    mine = 2 * OCT
    prod_out = []

    def send(places):
        for p in sorted(places, key=lambda p: abs((p + lead) % n_col * 2 - n_col)):
            d = (p + lead) % n_col
            if d:
                copy = pltpu.make_async_remote_copy(
                    src_ref=ps.at[:, pl.ds(p * mine, mine)], dst_ref=pr.at[c],
                    send_sem=p_send.at[d], recv_sem=p_recv.at[c], device_id=(r, lax.rem(c + d, n_col)),
                    device_id_type=MESH)
                copy.start()
                prod_out.append(copy)

    if small:
        for half in range(2):
            prod = jnp.dot(a[256 * half:256 * (half + 1), :], w[...], preferred_element_type=F32)
            slabs = [prod[16 * n:16 * n + 8] + prod[16 * n + 8:16 * n + 16] for n in range(2 * OCT)]
            for g in range(OCT):
                put(8 * half, g, slabs[g], slabs[OCT + g])
            send(range(4 * half, 4 * half + 4))
    else:
        for g in range(OCT):
            def add(j, acc, g=g):
                hi, lo = dense(live(j * tile_rows, tile_rows), g)
                lhs = jnp.concatenate([hi[:, :256], hi[:, 256:], lo[:, :256], lo[:, 256:]], axis=0).astype(BF16)
                return acc + jnp.dot(lhs, w[pl.ds(pl.multiple_of(j * 256, 256), 256), :], preferred_element_type=F32)
            acc = lax.fori_loop(0, tile_cols, add, jnp.zeros((4 * tile_rows, 256), F32))
            acc = acc[:2 * tile_rows] + acc[2 * tile_rows:]
            put(0, g, acc[:tile_rows], acc[tile_rows:])
        send(range(n_col))

    own = iota((128, 128), 0)
    wanted = (own & 15) * 8 + lax.shift_right_logical(own, 4)
    res_rows = jnp.where(iota((128, 128), 1) == wanted, jnp.broadcast_to(res_ref[...].reshape(1, 128), (128, 128)), 0.0)
    at_k = (iota((128, 128), 1) == K).astype(F32).astype(BF16)
    res_col = jnp.zeros((128, 128), F32)
    for piece in reversed(pieces(res_rows)):
        res_col += jnp.dot(piece, at_k, preferred_element_type=F32)
    product = ps[:, (n_col - lead) * mine:(n_col - lead + 1) * mine, :]
    for d in range(1, n_col):
        source = lax.rem(c + d, n_col)
        pltpu.make_async_remote_copy(
            src_ref=ps.at[:, pl.ds(0, mine)], dst_ref=pr.at[source], send_sem=p_send.at[d], recv_sem=p_recv.at[source],
            device_id=(r, source), device_id_type=MESH).wait_recv()
        product += pr[source]
    product = jnp.concatenate([product[0], product[1], product[2]], axis=1)

    lane = iota((2 * OCT, 128), 1)
    turned = [product if b == 0 else pltpu.roll(product, WIDE - K * b, 1) for b in range(8)]
    stacked = jnp.concatenate([jnp.where(lane < K, t[:, :128], 0.0) for t in turned], axis=0) + res_col
    hi, mid, lo = pieces(stacked)
    gram = lax.dot_general(
        jnp.concatenate([lo, hi, mid, mid, hi, hi], axis=0)[:, :SIDE],
        jnp.concatenate([hi, lo, mid, hi, mid, hi], axis=0), (((0,), (0,)), ((), ())), preferred_element_type=F32)
    parts = [gram[16 * n:16 * (n + 1)] for n in range(3)]
    packed = parts[0]
    for first, n, by in ((16, 1, 16), (48, 2, 48), (96, 0, 48), (97, 1, 49), (98, 2, 50)):
        packed = jnp.where(lane >= first, pltpu.roll(parts[n], by, 1), packed)

    pair, side = c // 2, lax.rem(c, 2)
    place_a = r * 2 + side
    ga[place_a] = packed
    sent = []
    others = []
    for d in range(2 * n_row):
        if d:
            row_to = lax.rem(r + d // 2, n_row)
            side_to = lax.rem(side + d % 2, 2)
            others.append((row_to * 2 + side_to, row_to, pair * 2 + side_to))
    for d, (slot, row_to, col_to) in enumerate(others):
        copy = pltpu.make_async_remote_copy(
            src_ref=ga.at[place_a], dst_ref=ga.at[place_a], send_sem=ga_send.at[d], recv_sem=ga_recv.at[place_a],
            device_id=(row_to, col_to), device_id_type=MESH)
        copy.start()
        sent.append(copy)
    for d, (slot, row_to, col_to) in enumerate(others):
        pltpu.make_async_remote_copy(
            src_ref=ga.at[place_a], dst_ref=ga.at[slot], send_sem=ga_send.at[d], recv_sem=ga_recv.at[slot],
            device_id=(row_to, col_to), device_id_type=MESH).wait_recv()
    packed = ga[0]
    for q in range(1, 2 * n_row):
        packed += ga[q]
    gb[pair] = packed
    pairs = n_col // 2
    for d in range(1, pairs):
        to = lax.rem(pair + d, pairs) * 2 + side
        copy = pltpu.make_async_remote_copy(
            src_ref=gb.at[pair], dst_ref=gb.at[pair], send_sem=gb_send.at[d], recv_sem=gb_recv.at[pair],
            device_id=(r, to), device_id_type=MESH)
        copy.start()
        sent.append(copy)
    own = xr[r].astype(F32)
    for t in range(3):
        out_ref[16 * t:16 * (t + 1), :] = product[:, 128 * t:128 * (t + 1)]
        out_ref[48 + 16 * t:64 + 16 * t, :] = own[:, 128 * t:128 * (t + 1)]
    for d in range(1, pairs):
        source = lax.rem(pair + d, pairs)
        pltpu.make_async_remote_copy(
            src_ref=gb.at[pair], dst_ref=gb.at[source], send_sem=gb_send.at[d], recv_sem=gb_recv.at[source],
            device_id=(r, source * 2 + side), device_id_type=MESH).wait_recv()
    packed = gb[0]
    for q in range(1, pairs):
        packed += gb[q]
    out_ref[96:112, :] = packed

    for copy in basis_out + prod_out + sent:
        copy.wait_send()


def eliminate(tiles):
    sub = iota((8, 128), 0)
    done = []
    for t0 in range(K // 8):
        j = 8 * t0
        cols = [[jnp.broadcast_to(tiles[t][:, j + k:j + k + 1], (8, 128)) for t in range(t0, K // 8)] for k in range(8)]
        rows = [jnp.broadcast_to(tiles[t0][i:i + 1, :], (8, 128)) for i in range(8)]
        s = [[jnp.broadcast_to(cols[k][0][i:i + 1, :], (8, 128)) if i >= k else None for k in range(8)] for i in range(8)]
        inv = []
        scale = jnp.zeros((8, 128), F32)
        for k in range(8):
            inv.append(1.0 / s[k][k])
            scale = jnp.where(sub == k, lax.rsqrt(s[k][k]), scale)
            for i in range(k + 1, 8):
                low = s[i][k] * inv[k]
                rows[i] = rows[i] - low * rows[k]
                for n in range(1, K // 8 - t0):
                    cols[i][n] = cols[i][n] - cols[k][n] * low
                for i2 in range(i, 8):
                    s[i2][i] = s[i2][i] - s[i2][k] * low
        for n in range(1, K // 8 - t0):
            gone = cols[0][n] * (rows[0] * inv[0])
            for k in range(1, 8):
                gone = gone + cols[k][n] * (rows[k] * inv[k])
            tiles[t0 + n] = tiles[t0 + n] - gone
        mixed = rows[0]
        for k in range(1, 8):
            mixed = jnp.where(sub == k, rows[k], mixed)
        done.append(mixed * scale)
    return jnp.concatenate(done, axis=0)


def finish(total, in_hbm, c_ref, u_ref, coef_ref, in_ref, sem):
    load = pltpu.make_async_copy(in_hbm, in_ref, sem)
    load.start()
    row_id = iota((K, 128), 0)
    lane_id = iota((K, 128), 1)
    tile_row = iota((128, WIDE), 0)
    tile_col = iota((128, WIDE), 1)
    tile = (tile_row - SIDE == tile_col - K * over_k(tile_col, 8)).astype(F32).astype(BF16)
    diag_row = over_k(iota((K, WIDE), 1), 8)
    load.wait()
    packed = in_ref[96:112, :] * F32(1.0 / total)
    low = jnp.concatenate([packed if by == 0 else pltpu.roll(packed, 128 - by, 1) for by in (0, 16, 48)], axis=0)
    beside = jnp.concatenate([pltpu.roll(packed, 128 - by, 1) for by in (48, 49, 50)], axis=0)
    high = jnp.concatenate([low, jnp.zeros((128 - K, 128), F32)], axis=0).T[:K]
    m = jnp.where(lane_id <= (row_id | 15), low, high)
    m = jnp.where(lane_id == K, beside, m)
    m = jnp.where(lane_id < SIDE, m, (lane_id - SIDE == row_id).astype(F32))
    m = eliminate([m[8 * t:8 * (t + 1)] for t in range(K // 8)])
    coef = jnp.broadcast_to(m[:, K:K + 1], (K, 128)) * F32(math.sqrt(total))
    coef_ref[...] = jnp.sum(jnp.where(lane_id == row_id, coef, 0.0), axis=0, keepdims=True)[:, :K]

    mine = 2 * OCT
    inverse = jnp.where(lane_id >= SIDE, m, 0.0)
    product, own = (
        jnp.concatenate([in_ref[first + 16 * t:first + 16 * (t + 1), :] for t in range(3)], axis=1) for first in (0, 48))
    left = jnp.concatenate(list(pieces(product)) + [own.astype(BF16)], axis=0)
    acc = [None, None]
    for n, piece in enumerate(pieces(inverse)):
        wide = jnp.dot(piece, tile, preferred_element_type=F32)
        big = jnp.concatenate([jnp.where(diag_row == b, wide, 0.0) for b in range(8)], axis=0).astype(BF16)
        out = lax.dot_general(left, big, (((1,), (1,)), ((), ())), preferred_element_type=F32)
        c_part = out[0:mine]
        for extra in range(1, 3 - n):
            c_part = c_part + out[extra * mine:(extra + 1) * mine]
        u_part = out[3 * mine:4 * mine]
        acc = [c_part, u_part] if n == 0 else [acc[0] + c_part, acc[1] + u_part]
    for ref, whole in ((c_ref, acc[0]), (u_ref, acc[1])):
        ref[...] = jnp.concatenate(
            [jnp.concatenate([whole[g:g + 1], whole[OCT + g:OCT + g + 1]], axis=0) for g in range(OCT)], axis=1
        ).astype(BF16)


def per_device(n_row, n_col, tangent, block_row, block_col, tile_count, old_basis, old_id, residual):
    stored = tangent.shape[2]
    tile_rows = 2 * n_col
    tile_cols = 2 * n_row
    small = tile_cols <= 8 and tile_rows == 16
    vmem = pl.BlockSpec(memory_space=pltpu.VMEM)
    dma = pltpu.SemaphoreType.DMA
    shares = pl.pallas_call(
        functools.partial(kernel, n_row, n_col, tile_rows, tile_cols),
        out_shape=jax.ShapeDtypeStruct((112, 128), F32),
        in_specs=[pl.BlockSpec(memory_space=pltpu.HBM)] * 7,
        out_specs=vmem,
        scratch_shapes=[
            pltpu.VMEM((stored, BLK * BLK), BF16),
            pltpu.VMEM((1, 1, stored), jnp.int32),
            pltpu.VMEM((1, 1, stored), jnp.int32),
            pltpu.SMEM((1, 1), jnp.int32),
            pltpu.VMEM((2, BLK * K), BF16),
            pltpu.SMEM((2,), jnp.int32),
            pltpu.VMEM((2 * BLK,), F32),
            pltpu.VMEM((2 * OCT, WIDE), BF16),
            pltpu.VMEM((n_row, 2 * OCT, WIDE), BF16),
            pltpu.VMEM((tile_cols * 256, 256), BF16),
            pltpu.VMEM((4 * OCT * tile_rows, tile_cols * 256) if small else (16, 128), BF16),
            pltpu.VMEM((3, OCT * tile_rows, 128), F32),
            pltpu.VMEM((n_col, 3, 2 * OCT, 128), F32),
            pltpu.VMEM((2 * n_row, 16, 128), F32),
            pltpu.VMEM((n_col // 2, 16, 128), F32),
            dma((7,)), dma((n_row,)), dma((n_row,)), dma((n_col,)), dma((n_col,)),
            dma((2 * n_row,)), dma((2 * n_row,)), dma((n_col // 2,)), dma((n_col // 2,)),
        ],
        compiler_params=pltpu.CompilerParams(
            collective_id=0, has_side_effects=True, vmem_limit_bytes=64 * 1024 * 1024),
        name="reduce",
    )(tangent, block_row, block_col, tile_count, old_basis, old_id, residual)
    recycled_c, recycled_u, coefficients = pl.pallas_call(
        functools.partial(finish, n_row * n_col * 2 * BLK),
        out_shape=(
            jax.ShapeDtypeStruct((2, BLK * K), BF16),
            jax.ShapeDtypeStruct((2, BLK * K), BF16),
            jax.ShapeDtypeStruct((1, K), F32),
        ),
        in_specs=[pl.BlockSpec(memory_space=pltpu.HBM)],
        out_specs=(vmem, vmem, vmem),
        scratch_shapes=[pltpu.VMEM((112, 128), F32), dma],
        compiler_params=pltpu.CompilerParams(vmem_limit_bytes=64 * 1024 * 1024),
        name="finish",
    )(shares)
    return recycled_c, recycled_u, coefficients[0]


def solution(mesh):
    return jax.shard_map(
        functools.partial(per_device, mesh.shape["row"], mesh.shape["col"]),
        mesh=mesh,
        in_specs=(
            P("row", "col", None, None),
            P("row", "col", None),
            P("row", "col", None),
            P("row", "col"),
            P(("row", "col"), None),
            P(("row", "col")),
            P(("row", "col")),
        ),
        out_specs=(P(("row", "col"), None), P(("row", "col"), None), P()),
        check_vma=False,
    )
```

```python
import functools
import math

import jax
import jax.numpy as jnp
from jax import lax
from jax.experimental import pallas as pl
from jax.experimental.pallas import tpu as pltpu
from jax.sharding import PartitionSpec as P

BLK = 64
K = 48
OCT = BLK // 8
WIDE = 8 * K
SIDE = 64
MESH = pl.DeviceIdType.MESH
F32 = jnp.float32
BF16 = jnp.bfloat16


def iota(shape, dim):
    return lax.broadcasted_iota(jnp.int32, shape, dim)


def over_k(index, most):
    whole = jnp.zeros_like(index)
    for step in range(1, most):
        whole += (index >= K * step).astype(jnp.int32)
    return whole


def pieces(x):
    hi = x.astype(BF16)
    rest = x - hi.astype(F32)
    mid = rest.astype(BF16)
    lo = (rest - mid.astype(F32)).astype(BF16)
    return hi, mid, lo


def kernel(n_row, n_col, tile_rows, tile_cols, tan_hbm, rows_hbm, cols_hbm, count_hbm, basis_hbm, id_hbm,
           res_hbm, out_ref,
           tan, rows_ref, cols_ref, count_ref, basis_ref, id_ref, res_ref, xs, xr, w, a, ps, pr, ga, gb,
           load_sem, bs_send, bs_recv, p_send, p_recv, ga_send, ga_recv, gb_send, gb_recv):
    r = lax.axis_index("row")
    c = lax.axis_index("col")
    nxt = lax.rem(c + 1, n_col)
    prv = lax.rem(c + n_col - 1, n_col)
    small = tile_cols <= 8 and tile_rows == 16
    lead = n_col // 4

    loads = [pltpu.make_async_copy(src, dst, load_sem.at[n]) for n, (src, dst) in enumerate((
        (basis_hbm, basis_ref), (id_hbm, id_ref), (tan_hbm.at[0, 0], tan), (rows_hbm, rows_ref),
        (cols_hbm, cols_ref), (count_hbm, count_ref), (res_hbm, res_ref)))]
    for load in loads:
        load.start()

    barrier = pltpu.get_barrier_semaphore()
    greeted = 0
    for d in range(1, n_row):
        other = lax.rem(r + d, n_row)
        for to in (c, nxt, prv):
            pl.semaphore_signal(barrier, inc=1, device_id=(other, to), device_id_type=MESH)
            greeted += 1
    for d in range(1, n_col):
        pl.semaphore_signal(barrier, inc=1, device_id=(r, lax.rem(c + d, n_col)), device_id_type=MESH)
        greeted += 1

    lane_k = over_k(iota((8, WIDE), 1), 8)
    own_lane = lane_k == iota((8, WIDE), 0)
    spread_row = iota((WIDE, 256), 0)
    spread_col = iota((WIDE, 256), 1)
    spread = jnp.logical_and(
        spread_row - K * over_k(spread_row, 8) == spread_col - K * over_k(spread_col, 4),
        spread_col < 4 * K).astype(F32).astype(BF16)
    quarter = over_k(iota((BLK, 256), 1), 5)

    loads[0].wait()
    loads[1].wait()
    flat = basis_ref[...].astype(F32)
    held = [jnp.concatenate([flat[s:s + 1, WIDE * g:WIDE * (g + 1)] for g in range(OCT)], axis=0) for s in range(2)]
    swapped = jnp.full((OCT, WIDE), id_ref[0] & 1, jnp.int32) == 1
    xs[...] = jnp.concatenate(
        [jnp.where(swapped, held[1], held[0]), jnp.where(swapped, held[0], held[1])], axis=0
    ).astype(BF16)

    pl.semaphore_wait(barrier, greeted)
    basis_out = []
    for d in range(n_row):
        to = lax.rem(r + d, n_row)
        copy = pltpu.make_async_remote_copy(
            src_ref=xs, dst_ref=xr.at[r], send_sem=bs_send.at[d], recv_sem=bs_recv.at[r],
            device_id=(to, nxt), device_id_type=MESH)
        copy.start()
        basis_out.append(copy)

    for load in loads[2:]:
        load.wait()
    stored = tan.shape[0]
    turned_row = rows_ref[0] - 2 * lax.rem(c + lead, n_col)
    place = cols_ref[0] * tile_rows + jnp.where(turned_row < 0, turned_row + tile_rows, turned_row)
    place = jnp.where(iota((1, stored), 1) < count_ref[0, 0], place, -1)

    def live(first, many):
        return (iota((many, stored), 0) + first == place).astype(F32).astype(BF16)

    def dense(hot, g):
        d = jnp.dot(hot, tan[:, 512 * g:512 * (g + 1)], preferred_element_type=F32)
        hi = d.astype(BF16).astype(F32)
        return hi, d - hi

    if small:
        hot = live(0, tile_cols * tile_rows)
        for g in range(OCT):
            hi, lo = dense(hot, g)
            for half in range(2):
                for h in range(2):
                    at = ((half * 2 + h) * OCT + g) * 16
                    for j in range(tile_cols):
                        take = (slice(16 * j + 8 * half, 16 * j + 8 * half + 8), slice(256 * h, 256 * (h + 1)))
                        a[at:at + 16, 256 * j:256 * (j + 1)] = jnp.concatenate([hi[take], lo[take]], axis=0).astype(BF16)

    for q in range(n_row):
        pltpu.make_async_remote_copy(
            src_ref=xs, dst_ref=xr.at[q], send_sem=bs_send.at[0], recv_sem=bs_recv.at[q],
            device_id=(r, nxt), device_id_type=MESH).wait_recv()

    for q in range(n_row):
        blocks = xr[q].astype(F32)
        opened = jnp.concatenate(
            [jnp.where(own_lane, jnp.broadcast_to(blocks[s:s + 1], (8, WIDE)), 0.0) for s in range(2 * OCT)],
            axis=0).astype(BF16)
        wide = jnp.dot(opened, spread, preferred_element_type=F32)
        for m in range(2):
            for e in range(4):
                at = (2 * q + m) * 256 + e * BLK
                w[at:at + BLK, :] = jnp.where(quarter == e, wide[BLK * m:BLK * (m + 1)], 0.0).astype(BF16)

    def put(first, g, left, right):
        turned = pltpu.roll(right, 64, 1)
        row = pl.ds(first * OCT + g, left.shape[0], stride=OCT)
        ps[0, row, :] = left[:, 0:128]
        ps[1, row, :] = left[:, 128:256] + turned[:, 0:128]
        ps[2, row, :] = turned[:, 128:256]

    mine = 2 * OCT
    prod_out = []

    def send(places):
        for p in sorted(places, key=lambda p: abs((p + lead) % n_col * 2 - n_col)):
            d = (p + lead) % n_col
            if d:
                copy = pltpu.make_async_remote_copy(
                    src_ref=ps.at[:, pl.ds(p * mine, mine)], dst_ref=pr.at[c],
                    send_sem=p_send.at[d], recv_sem=p_recv.at[c], device_id=(r, lax.rem(c + d, n_col)),
                    device_id_type=MESH)
                copy.start()
                prod_out.append(copy)

    if small:
        for half in range(2):
            prod = jnp.dot(a[256 * half:256 * (half + 1), :], w[...], preferred_element_type=F32)
            slabs = [prod[16 * n:16 * n + 8] + prod[16 * n + 8:16 * n + 16] for n in range(2 * OCT)]
            for g in range(OCT):
                put(8 * half, g, slabs[g], slabs[OCT + g])
            send(range(4 * half, 4 * half + 4))
    else:
        for g in range(OCT):
            def add(j, acc, g=g):
                hi, lo = dense(live(j * tile_rows, tile_rows), g)
                lhs = jnp.concatenate([hi[:, :256], hi[:, 256:], lo[:, :256], lo[:, 256:]], axis=0).astype(BF16)
                return acc + jnp.dot(lhs, w[pl.ds(pl.multiple_of(j * 256, 256), 256), :], preferred_element_type=F32)
            acc = lax.fori_loop(0, tile_cols, add, jnp.zeros((4 * tile_rows, 256), F32))
            acc = acc[:2 * tile_rows] + acc[2 * tile_rows:]
            put(0, g, acc[:tile_rows], acc[tile_rows:])
        send(range(n_col))

    own = iota((128, 128), 0)
    wanted = (own & 15) * 8 + lax.shift_right_logical(own, 4)
    res_rows = jnp.where(iota((128, 128), 1) == wanted, jnp.broadcast_to(res_ref[...].reshape(1, 128), (128, 128)), 0.0)
    at_k = (iota((128, 128), 1) == K).astype(F32).astype(BF16)
    res_col = jnp.zeros((128, 128), F32)
    for piece in reversed(pieces(res_rows)):
        res_col += jnp.dot(piece, at_k, preferred_element_type=F32)
    product = ps[:, (n_col - lead) * mine:(n_col - lead + 1) * mine, :]
    for d in range(1, n_col):
        source = lax.rem(c + d, n_col)
        pltpu.make_async_remote_copy(
            src_ref=ps.at[:, pl.ds(0, mine)], dst_ref=pr.at[source], send_sem=p_send.at[d], recv_sem=p_recv.at[source],
            device_id=(r, source), device_id_type=MESH).wait_recv()
        product += pr[source]
    product = jnp.concatenate([product[0], product[1], product[2]], axis=1)

    lane = iota((2 * OCT, 128), 1)
    turned = [product if b == 0 else pltpu.roll(product, WIDE - K * b, 1) for b in range(8)]
    stacked = jnp.concatenate([jnp.where(lane < K, t[:, :128], 0.0) for t in turned], axis=0) + res_col
    hi, mid, lo = pieces(stacked)
    gram = lax.dot_general(
        jnp.concatenate([lo, hi, mid, mid, hi, hi], axis=0)[:, :SIDE],
        jnp.concatenate([hi, lo, mid, hi, mid, hi], axis=0), (((0,), (0,)), ((), ())), preferred_element_type=F32)
    parts = [gram[16 * n:16 * (n + 1)] for n in range(3)]
    packed = parts[0]
    for first, n, by in ((16, 1, 16), (48, 2, 48), (96, 0, 48), (97, 1, 49), (98, 2, 50)):
        packed = jnp.where(lane >= first, pltpu.roll(parts[n], by, 1), packed)

    pair, side = c // 2, lax.rem(c, 2)
    place_a = r * 2 + side
    ga[place_a] = packed
    sent = []
    others = []
    for d in range(2 * n_row):
        if d:
            row_to = lax.rem(r + d // 2, n_row)
            side_to = lax.rem(side + d % 2, 2)
            others.append((row_to * 2 + side_to, row_to, pair * 2 + side_to))
    for d, (slot, row_to, col_to) in enumerate(others):
        copy = pltpu.make_async_remote_copy(
            src_ref=ga.at[place_a], dst_ref=ga.at[place_a], send_sem=ga_send.at[d], recv_sem=ga_recv.at[place_a],
            device_id=(row_to, col_to), device_id_type=MESH)
        copy.start()
        sent.append(copy)
    for d, (slot, row_to, col_to) in enumerate(others):
        pltpu.make_async_remote_copy(
            src_ref=ga.at[place_a], dst_ref=ga.at[slot], send_sem=ga_send.at[d], recv_sem=ga_recv.at[slot],
            device_id=(row_to, col_to), device_id_type=MESH).wait_recv()
    packed = ga[0]
    for q in range(1, 2 * n_row):
        packed += ga[q]
    gb[pair] = packed
    pairs = n_col // 2
    for d in range(1, pairs):
        to = lax.rem(pair + d, pairs) * 2 + side
        copy = pltpu.make_async_remote_copy(
            src_ref=gb.at[pair], dst_ref=gb.at[pair], send_sem=gb_send.at[d], recv_sem=gb_recv.at[pair],
            device_id=(r, to), device_id_type=MESH)
        copy.start()
        sent.append(copy)
    own = xr[r].astype(F32)
    for t in range(3):
        out_ref[16 * t:16 * (t + 1), :] = product[:, 128 * t:128 * (t + 1)]
        out_ref[48 + 16 * t:64 + 16 * t, :] = own[:, 128 * t:128 * (t + 1)]
    for d in range(1, pairs):
        source = lax.rem(pair + d, pairs)
        pltpu.make_async_remote_copy(
            src_ref=gb.at[pair], dst_ref=gb.at[source], send_sem=gb_send.at[d], recv_sem=gb_recv.at[source],
            device_id=(r, source * 2 + side), device_id_type=MESH).wait_recv()
    packed = gb[0]
    for q in range(1, pairs):
        packed += gb[q]
    out_ref[96:112, :] = packed

    for copy in basis_out + prod_out + sent:
        copy.wait_send()


def eliminate(tiles):
    sub = iota((8, 128), 0)
    done = []
    for t0 in range(K // 8):
        j = 8 * t0
        cols = [[jnp.broadcast_to(tiles[t][:, j + k:j + k + 1], (8, 128)) for t in range(t0, K // 8)] for k in range(8)]
        rows = [jnp.broadcast_to(tiles[t0][i:i + 1, :], (8, 128)) for i in range(8)]
        s = [[jnp.broadcast_to(cols[k][0][i:i + 1, :], (8, 128)) if i >= k else None for k in range(8)] for i in range(8)]
        inv = []
        scale = jnp.zeros((8, 128), F32)
        for k in range(8):
            inv.append(1.0 / s[k][k])
            scale = jnp.where(sub == k, lax.rsqrt(s[k][k]), scale)
            for i in range(k + 1, 8):
                low = s[i][k] * inv[k]
                rows[i] = rows[i] - low * rows[k]
                for n in range(1, K // 8 - t0):
                    cols[i][n] = cols[i][n] - cols[k][n] * low
                for i2 in range(i, 8):
                    s[i2][i] = s[i2][i] - s[i2][k] * low
        for n in range(1, K // 8 - t0):
            gone = cols[0][n] * (rows[0] * inv[0])
            for k in range(1, 8):
                gone = gone + cols[k][n] * (rows[k] * inv[k])
            tiles[t0 + n] = tiles[t0 + n] - gone
        mixed = rows[0]
        for k in range(1, 8):
            mixed = jnp.where(sub == k, rows[k], mixed)
        done.append(mixed * scale)
    return jnp.concatenate(done, axis=0)


def finish(total, in_hbm, c_ref, u_ref, coef_ref, in_ref, sem):
    load = pltpu.make_async_copy(in_hbm, in_ref, sem)
    load.start()
    row_id = iota((K, 128), 0)
    lane_id = iota((K, 128), 1)
    tile_row = iota((128, WIDE), 0)
    tile_col = iota((128, WIDE), 1)
    tile = (tile_row - SIDE == tile_col - K * over_k(tile_col, 8)).astype(F32).astype(BF16)
    diag_row = over_k(iota((K, WIDE), 1), 8)
    load.wait()
    packed = in_ref[96:112, :] * F32(1.0 / total)
    low = jnp.concatenate([packed if by == 0 else pltpu.roll(packed, 128 - by, 1) for by in (0, 16, 48)], axis=0)
    beside = jnp.concatenate([pltpu.roll(packed, 128 - by, 1) for by in (48, 49, 50)], axis=0)
    high = jnp.concatenate([low, jnp.zeros((128 - K, 128), F32)], axis=0).T[:K]
    m = jnp.where(lane_id <= (row_id | 15), low, high)
    m = jnp.where(lane_id == K, beside, m)
    m = jnp.where(lane_id < SIDE, m, (lane_id - SIDE == row_id).astype(F32))
    m = eliminate([m[8 * t:8 * (t + 1)] for t in range(K // 8)])
    coef = jnp.broadcast_to(m[:, K:K + 1], (K, 128)) * F32(math.sqrt(total))
    coef_ref[...] = jnp.sum(jnp.where(lane_id == row_id, coef, 0.0), axis=0, keepdims=True)[:, :K]

    mine = 2 * OCT
    inverse = jnp.where(lane_id >= SIDE, m, 0.0)
    product, own = (
        jnp.concatenate([in_ref[first + 16 * t:first + 16 * (t + 1), :] for t in range(3)], axis=1) for first in (0, 48))
    left = jnp.concatenate(list(pieces(product)) + [own.astype(BF16)], axis=0)
    acc = [None, None]
    for n, piece in enumerate(pieces(inverse)):
        wide = jnp.dot(piece, tile, preferred_element_type=F32)
        big = jnp.concatenate([jnp.where(diag_row == b, wide, 0.0) for b in range(8)], axis=0).astype(BF16)
        out = lax.dot_general(left, big, (((1,), (1,)), ((), ())), preferred_element_type=F32)
        c_part = out[0:mine]
        for extra in range(1, 3 - n):
            c_part = c_part + out[extra * mine:(extra + 1) * mine]
        u_part = out[3 * mine:4 * mine]
        acc = [c_part, u_part] if n == 0 else [acc[0] + c_part, acc[1] + u_part]
    for ref, whole in ((c_ref, acc[0]), (u_ref, acc[1])):
        ref[...] = jnp.concatenate(
            [jnp.concatenate([whole[g:g + 1], whole[OCT + g:OCT + g + 1]], axis=0) for g in range(OCT)], axis=1
        ).astype(BF16)


def per_device(n_row, n_col, tangent, block_row, block_col, tile_count, old_basis, old_id, residual):
    stored = tangent.shape[2]
    tile_rows = 2 * n_col
    tile_cols = 2 * n_row
    small = tile_cols <= 8 and tile_rows == 16
    vmem = pl.BlockSpec(memory_space=pltpu.VMEM)
    dma = pltpu.SemaphoreType.DMA
    shares = pl.pallas_call(
        functools.partial(kernel, n_row, n_col, tile_rows, tile_cols),
        out_shape=jax.ShapeDtypeStruct((112, 128), F32),
        in_specs=[pl.BlockSpec(memory_space=pltpu.HBM)] * 7,
        out_specs=vmem,
        scratch_shapes=[
            pltpu.VMEM((stored, BLK * BLK), BF16),
            pltpu.VMEM((1, 1, stored), jnp.int32),
            pltpu.VMEM((1, 1, stored), jnp.int32),
            pltpu.SMEM((1, 1), jnp.int32),
            pltpu.VMEM((2, BLK * K), BF16),
            pltpu.SMEM((2,), jnp.int32),
            pltpu.VMEM((2 * BLK,), F32),
            pltpu.VMEM((2 * OCT, WIDE), BF16),
            pltpu.VMEM((n_row, 2 * OCT, WIDE), BF16),
            pltpu.VMEM((tile_cols * 256, 256), BF16),
            pltpu.VMEM((4 * OCT * tile_rows, tile_cols * 256) if small else (16, 128), BF16),
            pltpu.VMEM((3, OCT * tile_rows, 128), F32),
            pltpu.VMEM((n_col, 3, 2 * OCT, 128), F32),
            pltpu.VMEM((2 * n_row, 16, 128), F32),
            pltpu.VMEM((n_col // 2, 16, 128), F32),
            dma((7,)), dma((n_row,)), dma((n_row,)), dma((n_col,)), dma((n_col,)),
            dma((2 * n_row,)), dma((2 * n_row,)), dma((n_col // 2,)), dma((n_col // 2,)),
        ],
        compiler_params=pltpu.CompilerParams(
            collective_id=0, has_side_effects=True, vmem_limit_bytes=54900 * 1024),
        name="reduce",
    )(tangent, block_row, block_col, tile_count, old_basis, old_id, residual)
    recycled_c, recycled_u, coefficients = pl.pallas_call(
        functools.partial(finish, n_row * n_col * 2 * BLK),
        out_shape=(
            jax.ShapeDtypeStruct((2, BLK * K), BF16),
            jax.ShapeDtypeStruct((2, BLK * K), BF16),
            jax.ShapeDtypeStruct((1, K), F32),
        ),
        in_specs=[pl.BlockSpec(memory_space=pltpu.HBM)],
        out_specs=(vmem, vmem, vmem),
        scratch_shapes=[pltpu.VMEM((112, 128), F32), dma],
        compiler_params=pltpu.CompilerParams(vmem_limit_bytes=16 * 1024 * 1024),
        name="finish",
    )(shares)
    return recycled_c, recycled_u, coefficients[0]


def solution(mesh):
    return jax.shard_map(
        functools.partial(per_device, mesh.shape["row"], mesh.shape["col"]),
        mesh=mesh,
        in_specs=(
            P("row", "col", None, None),
            P("row", "col", None),
            P("row", "col", None),
            P("row", "col"),
            P(("row", "col"), None),
            P(("row", "col")),
            P(("row", "col")),
        ),
        out_specs=(P(("row", "col"), None), P(("row", "col"), None), P()),
        check_vma=False,
    )
```
